512 devices in a mesh: pair: 16 (over x, z_hi, core), stack: 32 (over y, z_lo).
Axes of the slice: x: 4, y: 4, z: 16 (z_hi: 2, z_lo: 8; z = z_hi * 8 + z_lo), core: 2. Of those that a mesh axis runs over, the one named last changes fastest.
Arguments:
- raw: bfloat16 [512, 64, 4096], P('stack', None, 'pair'), may hold values from -6 to 6
- valid: int32 [512, 16], P('stack', 'pair'), may hold values 0 or 1
- partners: int32 [4, 16], replicated, may hold values from 0 to 15, as said below
Outputs:
- correlations: bfloat16 [4, 4096, 64, 256], P(None, ('pair', 'stack'))
The draws below stay inside these ranges and needn't reach their ends.
Inputs may be any that keep to these rules, and one draw needn't show every extreme that they name: `partners`: each row couples all blocks in pairs: the partner of a block's partner is the block itself, and no block is its own partner.
All inputs are finite; a program needn't handle non-finite values. No bound on the sum of `valid` on one device may be relied on, other than what follows from the above.
Results may differ from the reference program's by a relative error of at most 0.0057.
Values may be sent and summed in bfloat16 or wider, within the bound.
A program may use at most 64 MiB of HBM per device.

```python
import math
import jax
import jax.numpy as jnp
from jax import lax

C = 256
SAMPLES = 64
ROUNDS = 4
WINDOWS = 512
CHANNELS = 4096
N_PAIR = 16


def draw_partners(key, part):
    key = jax.random.fold_in(key, 7)
    plan_rows = []
    for pairing in range(ROUNDS):
        shuffled = jax.random.permutation(jax.random.fold_in(key, pairing), N_PAIR).astype(jnp.int32)
        swapped = shuffled.reshape(-1, 2)[:, ::-1].reshape(-1)
        plan_rows.append(jnp.zeros((N_PAIR,), jnp.int32).at[shuffled].set(swapped))
    return jnp.stack(plan_rows).astype(jnp.int32)


def plant(drawn, rng, smallest, largest):
    longest = drawn.shape.index(max(drawn.shape))
    spots = []
    for shift in (0, 1):
        where = [jax.random.randint(jax.random.fold_in(rng, axis), (), 0, length) for axis, length in enumerate(drawn.shape)]
        where[longest] = (where[longest] + shift) % drawn.shape[longest]
        spots.append(tuple(where))
    return drawn.at[spots[0]].set(smallest).at[spots[1]].set(largest)


def block_levels(own_key, dims, shards, smallest, top_value):
    gain, own = 1.0, jax.random.fold_in(own_key, 6)
    for axis_at, parts in shards:
        heights = jnp.exp(jax.random.uniform(jax.random.fold_in(own, axis_at), (parts,), jnp.float32, smallest / len(shards), top_value / len(shards)))
        gain = gain * jnp.repeat(heights, dims[axis_at] // parts).reshape([-1 if axis == axis_at else 1 for axis in range(len(dims))])
    return gain


def normal_values(rng, extent, width, most, cuts=(), kind=jnp.bfloat16):
    gain = block_levels(rng, extent, cuts, -0.22, 0.18) if cuts else 1.0
    values = jax.random.normal(rng, extent, jnp.float32) * width * gain
    return jnp.minimum(jnp.maximum(values, -most), most).astype(kind)


def setup_inputs(seed: int = 0) -> dict:
    splits = jax.random.split(jax.random.key(seed), 4)
    raw = normal_values(splits[0], (WINDOWS, SAMPLES, CHANNELS), 1.0, 6.0, ((0, 32), (2, 16)))
    valid = plant((jax.random.randint(splits[1], (WINDOWS, N_PAIR), 0, 4) < 3).astype(jnp.int32), jax.random.fold_in(splits[1], 1), 0, 1)
    partners = draw_partners(jax.random.fold_in(splits[3], 71), 0)
    return dict(raw=raw, valid=valid, partners=partners)


epsilon = 1e-06

def forward_table(samples):
    sample_ids = jnp.arange(samples, dtype=jnp.int32)
    freq_ids = jnp.arange(1, samples // 2 + 1, dtype=jnp.int32)
    phases = (freq_ids[:, None] * sample_ids[None, :] % samples).astype(jnp.float32) * (2.0 * math.pi / samples)
    return jnp.stack([jnp.cos(phases), -jnp.sin(phases)], axis=1)

def lag_table(samples):
    shifts = jnp.arange(samples, dtype=jnp.int32) - samples // 2
    freq_ids = jnp.arange(1, samples // 2 + 1, dtype=jnp.int32)
    phases = (shifts[:, None] * freq_ids[None, :] % samples).astype(jnp.float32) * (2.0 * math.pi / samples)
    weights = jnp.where(freq_ids == samples // 2, 1.0, 2.0).astype(jnp.float32)[None, :]
    return jnp.stack([weights * jnp.cos(phases), -weights * jnp.sin(phases)], axis=-1)

def whiten(raw_blocks, valid, samples):
    spectra = jnp.einsum('fkt,wtbc->wfkbc', forward_table(samples), raw_blocks.astype(jnp.float32), precision=lax.Precision.HIGHEST)
    band_power = lax.optimization_barrier(jnp.mean(lax.optimization_barrier(jnp.sum(spectra * spectra, axis=2)), axis=-1))
    scaled = spectra * lax.rsqrt(band_power + epsilon)[:, :, None, :, None]
    return (scaled * valid.astype(jnp.float32)[:, None, None, :, None]).astype(jnp.bfloat16)

def reference(raw, valid, partners):
    whitened = whiten(raw.reshape(WINDOWS, SAMPLES, N_PAIR, C), valid, SAMPLES)
    blocks = jnp.moveaxis(whitened, 3, 0)
    lag_weights = lag_table(SAMPLES)

    def one_block(inputs):
        own_block, partner_id = inputs
        partner_block = lax.dynamic_index_in_dim(blocks, partner_id.astype(jnp.int32), 0, keepdims=False).astype(jnp.float32)
        own_wide = own_block.astype(jnp.float32)
        rotated = jnp.stack([own_wide[:, :, 1], -own_wide[:, :, 0]], axis=2)
        real_part = jnp.einsum('wfjc,wfjd->fcd', own_wide, partner_block)
        imag_part = jnp.einsum('wfjc,wfjd->fcd', rotated, partner_block)
        cross_spec = jnp.stack([real_part, imag_part], axis=1)
        lagged = jnp.einsum('lfj,fjcd->cld', lag_weights, cross_spec, precision=lax.Precision.HIGHEST) / WINDOWS
        return lagged.astype(jnp.bfloat16)
    outputs = []
    for pairing in range(ROUNDS):
        per_block = lax.map(one_block, (blocks, partners[pairing]))
        outputs.append(per_block.reshape(CHANNELS, SAMPLES, C))
    return jnp.stack(outputs)
```

```python
from functools import partial
import math

import jax
import jax.numpy as jnp
from jax import lax
from jax.experimental import pallas as pl
from jax.experimental.pallas import tpu as pltpu
from jax.sharding import PartitionSpec as P

epsilon = 1e-06
MESH = pl.DeviceIdType.MESH
X, Y, Z, ZL, CORES = 4, 4, 16, 8, 2


def forward_table(samples):
    sample_ids = jnp.arange(samples, dtype=jnp.int32)
    freq_ids = jnp.arange(1, samples // 2 + 1, dtype=jnp.int32)
    phases = (freq_ids[:, None] * sample_ids[None, :] % samples).astype(jnp.float32) * (
        2.0 * math.pi / samples
    )
    return jnp.stack([jnp.cos(phases), -jnp.sin(phases)], axis=1)


def lag_table(samples):
    shifts = jnp.arange(samples, dtype=jnp.int32) - samples // 2
    freq_ids = jnp.arange(1, samples // 2 + 1, dtype=jnp.int32)
    phases = (shifts[:, None] * freq_ids[None, :] % samples).astype(jnp.float32) * (
        2.0 * math.pi / samples
    )
    weights = jnp.where(freq_ids == samples // 2, 1.0, 2.0).astype(jnp.float32)[None, :]
    return jnp.stack([weights * jnp.cos(phases), weights * jnp.sin(phases)], axis=-1)


def whiten(raw, valid, samples):
    spectra = jnp.einsum(
        "fkt,wtc->wfkc",
        forward_table(samples),
        raw.astype(jnp.float32),
        precision=lax.Precision.HIGHEST,
    )
    band_power = jnp.mean(jnp.sum(spectra * spectra, axis=2), axis=-1)
    scaled = spectra * lax.rsqrt(band_power + epsilon)[:, :, None, None]
    return (scaled * valid.astype(jnp.float32)[:, None, None, None]).astype(jnp.bfloat16)


def place():
    pair, stack = lax.axis_index("pair"), lax.axis_index("stack")
    core = lax.rem(pair, 2)
    z_hi = lax.rem(lax.div(pair, 2), 2)
    return lax.div(pair, 4), lax.div(stack, ZL), z_hi * ZL + lax.rem(stack, ZL), core


def device(x, y, z, core):
    return (x * 4 + lax.div(z, ZL) * 2 + core, y * ZL + lax.rem(z, ZL))


def turn(index, by, size):
    return lax.rem(index + by, size)


def remote(src, dst, send, recv, to):
    return pltpu.make_async_remote_copy(
        src_ref=src, dst_ref=dst, send_sem=send, recv_sem=recv, device_id=to, device_id_type=MESH
    )


def gather_kernel(spec, rows, cols, landed, z_send, z_recv, x_send, x_recv, y_send, y_recv,
                  gx_send, gx_recv, gy_send, gy_recv, here):
    x, y, z, core = place()
    z_peers = [device(x, y, turn(z, by, Z), core) for by in range(1, Z)]
    x_steps = [(dx, dc) for dx in range(X) for dc in range(CORES) if dx or dc]
    x_peers = [device(turn(x, dx, X), y, z, turn(core, dc, CORES)) for dx, dc in x_steps]
    y_peers = [device(x, turn(y, dx, Y), z, turn(core, dc, CORES)) for dx, dc in x_steps]
    barrier = pltpu.get_barrier_semaphore()
    peers = z_peers + x_peers + y_peers[1:]
    for peer in peers:
        pl.semaphore_signal(barrier, inc=1, device_id=peer, device_id_type=MESH)
    pl.semaphore_wait(barrier, len(peers))

    copies = []
    for by in range(1, Z):
        to = turn(z, by, Z)
        copies.append(remote(spec.at[lax.div(to, ZL), lax.rem(to, ZL)],
                             landed.at[lax.div(z, ZL), lax.rem(z, ZL)],
                             z_send.at[by - 1], z_recv.at[by - 1], z_peers[by - 1]))
    for copy in copies:
        copy.start()
    own = pltpu.make_async_copy(spec.at[lax.div(z, ZL), lax.rem(z, ZL)],
                                landed.at[lax.div(z, ZL), lax.rem(z, ZL)], here.at[0])
    own.start()
    own.wait()
    for copy in copies:
        copy.wait()

    col_copies, row_copies = [], []
    for n, (dx, dc) in enumerate(x_steps):
        to_x, to_y, to_core = turn(x, dx, X), turn(y, dx, Y), turn(core, dc, CORES)
        col_copies.append(remote(landed.at[:, :, to_core, to_x], cols.at[x, :, core, y],
                                 x_send.at[n], x_recv.at[n], x_peers[n]))
        row_copies.append(remote(landed.at[:, :, to_core, to_y], rows.at[x, :, core, y],
                                 y_send.at[n], y_recv.at[n], y_peers[n]))
    for a, b in zip(col_copies, row_copies):
        a.start()
        b.start()
    col_own = pltpu.make_async_copy(landed.at[:, :, core, x], cols.at[x, :, core, y], here.at[0])
    row_own = pltpu.make_async_copy(landed.at[:, :, core, y], rows.at[x, :, core, y], here.at[1])
    col_own.start()
    row_own.start()
    col_own.wait()
    row_own.wait()
    for a, b in zip(col_copies, row_copies):
        a.wait()
        b.wait()

    x_next, x_prev = device(turn(x, 1, X), y, z, core), device(turn(x, 3, X), y, z, core)
    y_next, y_prev = device(x, turn(y, 1, Y), z, core), device(x, turn(y, 3, Y), z, core)
    first = [
        remote(rows.at[x], rows.at[x], gx_send.at[0], gx_recv.at[0], x_next),
        remote(cols.at[:, :, :, y], cols.at[:, :, :, y], gy_send.at[0], gy_recv.at[0], y_next),
        remote(rows.at[x], rows.at[x], gx_send.at[1], gx_recv.at[1], x_prev),
        remote(cols.at[:, :, :, y], cols.at[:, :, :, y], gy_send.at[1], gy_recv.at[1], y_prev),
    ]
    for copy in first:
        copy.start()
    xp, xn = turn(x, 3, X), turn(x, 1, X)
    yp, yn = turn(y, 3, Y), turn(y, 1, Y)
    second = [
        remote(rows.at[xp, 0], rows.at[xp, 0], gx_send.at[2], gx_recv.at[2], x_next),
        remote(cols.at[:, 0, :, yp], cols.at[:, 0, :, yp], gy_send.at[2], gy_recv.at[2], y_next),
        remote(rows.at[xn, 1], rows.at[xn, 1], gx_send.at[3], gx_recv.at[3], x_prev),
        remote(cols.at[:, 1, :, yn], cols.at[:, 1, :, yn], gy_send.at[3], gy_recv.at[3], y_prev),
    ]
    for a, b in zip(first, second):
        a.wait_recv()
        b.start()
    for a, b in zip(first, second):
        a.wait_send()
        b.wait()


def gather(spec):
    side = jax.ShapeDtypeStruct((X, 2, CORES, Y, ZL, 16, 128), jnp.bfloat16)
    sems = [15, 15, 7, 7, 7, 7, 4, 4, 4, 4, 2]
    vmem = pl.BlockSpec(memory_space=pltpu.VMEM)
    return pl.pallas_call(
        gather_kernel,
        out_shape=(side, side),
        in_specs=[vmem],
        out_specs=(vmem, vmem),
        scratch_shapes=[pltpu.VMEM((2, ZL, 2, 4, 16, 128), jnp.bfloat16)]
        + [pltpu.SemaphoreType.DMA((n,)) for n in sems],
        compiler_params=pltpu.CompilerParams(
            collective_id=0, has_side_effects=True, vmem_limit_bytes=40 << 20
        ),
        cost_estimate=pl.CostEstimate(flops=0, bytes_accessed=9 << 20, transcendentals=0),
    )(spec)


def cross_kernel(partners, rows, cols, out):
    lanes = lax.broadcasted_iota(jnp.int32, (64, 128), 1)
    sign = jnp.where(lanes < 64, 1.0, -1.0).astype(jnp.float32)

    def block(p, carry):
        own = rows[p]
        picked = jnp.concatenate([cols[partners[r, p]] for r in range(4)], axis=1)
        both = lax.dot_general(own, picked, (((0,), (0,)), ((), ())),
                               preferred_element_type=jnp.float32)
        parts = []
        for r in range(4):
            at = both[:, 128 * r:128 * (r + 1)]
            part = at[:64] + sign * pltpu.roll(at[64:], 64, 1)
            parts.append(part.reshape(8, 8, 128))
        out[p] = jnp.concatenate(parts, axis=1).astype(jnp.bfloat16)
        return carry

    lax.fori_loop(0, 16, block, 0)


def cross(partners, rows, cols):
    vmem = pl.BlockSpec(memory_space=pltpu.VMEM)
    return pl.pallas_call(
        cross_kernel,
        out_shape=jax.ShapeDtypeStruct((16, 8, 32, 128), jnp.bfloat16),
        in_specs=[pl.BlockSpec(memory_space=pltpu.SMEM), vmem, vmem],
        out_specs=vmem,
        compiler_params=pltpu.CompilerParams(vmem_limit_bytes=40 << 20),
        cost_estimate=pl.CostEstimate(flops=1 << 30, bytes_accessed=5 << 20, transcendentals=0),
    )(partners, rows.reshape(16, 512, 128), cols.reshape(16, 512, 128))


def spread_kernel(parts, out, send, recv, here):
    x, y, z, core = place()
    pair, low = lax.axis_index("pair"), lax.rem(lax.axis_index("stack"), ZL)

    def target(n):
        return turn(pair, lax.div(n, ZL), 16), turn(low, lax.rem(n, ZL), ZL)

    barrier = pltpu.get_barrier_semaphore()

    def greet(n, carry):
        p, zl = target(n)
        pl.semaphore_signal(barrier, inc=1, device_id=(p, y * ZL + zl), device_id_type=MESH)
        return carry

    lax.fori_loop(1, 128, greet, 0)
    pl.semaphore_wait(barrier, 127)

    def copy(n):
        p, zl = target(n)
        return remote(parts.at[p, zl], out.at[z, core, x], send.at[n - 1], recv.at[n - 1],
                      (p, y * ZL + zl))

    def start(n, carry):
        copy(n).start()
        return carry

    def finish(n, carry):
        copy(n).wait()
        return carry

    lax.fori_loop(1, 128, start, 0)
    own = pltpu.make_async_copy(parts.at[pair, low], out.at[z, core, x], here)
    own.start()
    own.wait()
    lax.fori_loop(1, 128, finish, 0)


def spread(parts):
    vmem = pl.BlockSpec(memory_space=pltpu.VMEM)
    return pl.pallas_call(
        spread_kernel,
        out_shape=jax.ShapeDtypeStruct((Z, CORES, X, 32, 128), jnp.bfloat16),
        in_specs=[vmem],
        out_specs=vmem,
        scratch_shapes=[pltpu.SemaphoreType.DMA((127,)), pltpu.SemaphoreType.DMA((127,)),
                        pltpu.SemaphoreType.DMA],
        compiler_params=pltpu.CompilerParams(
            collective_id=1, has_side_effects=True, vmem_limit_bytes=40 << 20
        ),
        cost_estimate=pl.CostEstimate(flops=0, bytes_accessed=2 << 20, transcendentals=0),
    )(parts)


def shards(raw, valid, partners):
    win_dev, samples, width = raw.shape
    whitened = whiten(raw, valid[:, 0], samples)
    spec = jnp.transpose(whitened.reshape(win_dev, 32, 2, 4, 64), (1, 3, 0, 2, 4))
    rows, cols = gather(spec.reshape(2, ZL, 2, 4, win_dev, 128))
    parts = cross(partners, rows, cols)
    got = spread(parts)
    got = got.reshape(32, 4, 4, 8, 2, 64).astype(jnp.float32)
    lagged = jnp.einsum("lfj,fgrcjd->rclgd", lag_table(samples), got, precision=lax.Precision.HIGHEST)
    return (lagged / 512).astype(jnp.bfloat16).reshape(4, 8, samples, 256)


def solution(mesh):
    return jax.shard_map(
        shards,
        mesh=mesh,
        in_specs=(P("stack", None, "pair"), P("stack", "pair"), P()),
        out_specs=P(None, ("pair", "stack"), None, None),
        check_vma=False,
    )
```

```python
from functools import partial
import math

import jax
import jax.numpy as jnp
from jax import lax
from jax.experimental import pallas as pl
from jax.experimental.pallas import tpu as pltpu
from jax.sharding import PartitionSpec as P

epsilon = 1e-06
MESH = pl.DeviceIdType.MESH
X, Y, Z, ZL, CORES = 4, 4, 16, 8, 2
ORDER = (1, 15, 2, 14, 3, 13, 4, 12, 5, 11, 6, 10, 7, 9, 8)
STEPS = (0, 1, 3, 2)


def forward_table(samples):
    sample_ids = jnp.arange(samples, dtype=jnp.int32)
    freq_ids = jnp.arange(1, samples // 2 + 1, dtype=jnp.int32)
    phases = (freq_ids[:, None] * sample_ids[None, :] % samples).astype(jnp.float32) * (
        2.0 * math.pi / samples
    )
    return jnp.stack([jnp.cos(phases), -jnp.sin(phases)], axis=1)


def lag_table(samples):
    shifts = jnp.arange(samples, dtype=jnp.int32) - samples // 2
    freq_ids = jnp.arange(1, samples // 2 + 1, dtype=jnp.int32)
    phases = (shifts[:, None] * freq_ids[None, :] % samples).astype(jnp.float32) * (
        2.0 * math.pi / samples
    )
    weights = jnp.where(freq_ids == samples // 2, 1.0, 2.0).astype(jnp.float32)[None, :]
    return jnp.stack([weights * jnp.cos(phases), weights * jnp.sin(phases)], axis=-1)


def whiten(raw, valid, samples):
    spectra = jnp.einsum(
        "fkt,wtc->wfkc",
        forward_table(samples),
        raw.astype(jnp.float32),
        precision=lax.Precision.HIGHEST,
    )
    band_power = jnp.mean(jnp.sum(spectra * spectra, axis=2), axis=-1)
    scaled = spectra * lax.rsqrt(band_power + epsilon)[:, :, None, None]
    return (scaled * valid.astype(jnp.float32)[:, None, None, None]).astype(jnp.bfloat16)


def place():
    pair, stack = lax.axis_index("pair"), lax.axis_index("stack")
    core = lax.rem(pair, 2)
    z_hi = lax.rem(lax.div(pair, 2), 2)
    return lax.div(pair, 4), lax.div(stack, ZL), z_hi * ZL + lax.rem(stack, ZL), core


def device(x, y, z, core):
    return (x * 4 + lax.div(z, ZL) * 2 + core, y * ZL + lax.rem(z, ZL))


def turn(index, by, size):
    return lax.rem(index + by, size)


def remote(src, dst, send, recv, to):
    return pltpu.make_async_remote_copy(
        src_ref=src, dst_ref=dst, send_sem=send, recv_sem=recv, device_id=to, device_id_type=MESH
    )


def local(src, dst, sem):
    return pltpu.make_async_copy(src, dst, sem)


def drain(ref, sem):
    pltpu.make_async_copy(ref, ref, sem).wait()


def exchange_kernel(partners, spec, out, landed, rows, cols_0, cols_1, parts, z_send, z_recv, xa_send, xa_recv,
                    ya_send, ya_recv, xg_send, xg_recv, yg_send, yg_recv, c_send, c_recv,
                    o_send, o_recv, here_z, here_x, here_y, here_o):
    x, y, z, core = place()
    cols = (cols_0, cols_1)
    z_hi, z_lo = lax.div(z, ZL), lax.rem(z, ZL)
    xs = [device(turn(x, d, X), y, z, core) for d in range(1, X)]
    ys = [device(x, turn(y, d, Y), z, core) for d in range(1, Y)]
    twin = device(x, y, z, 1 - core)

    def target(n):
        return (turn(x, lax.div(n, Z), X), turn(z_hi, lax.rem(lax.div(n, ZL), 2), 2),
                turn(z_lo, lax.rem(n, ZL), ZL))

    barrier = pltpu.get_barrier_semaphore()

    def greet(n, carry):
        tx, th, tl = target(n)
        pl.semaphore_signal(barrier, inc=1, device_id=device(tx, y, th * ZL + tl, core), device_id_type=MESH)
        return carry

    lax.fori_loop(1, 64, greet, 0)
    for peer in ys + [twin]:
        pl.semaphore_signal(barrier, inc=1, device_id=peer, device_id_type=MESH)
    pl.semaphore_wait(barrier, 67)

    quad = lax.div(z, 4)
    for chunk in range(2):
        local(spec.at[chunk, z], landed.at[chunk, z], here_z.at[chunk]).start()
        for by in ORDER:
            to = turn(z, by, Z)
            remote(spec.at[chunk, to], landed.at[chunk, z], z_send.at[chunk],
                   z_recv.at[chunk, quad], device(x, y, to, core)).start()

    def of_quad(q):
        return lax.div(q, 2), pl.ds(lax.rem(q, 2) * 4, 4)

    def to_groups(chunk, step):
        q = turn(quad, step, 4)
        hi, lo = of_quad(q)
        zs = pl.ds(q * 4, 4)
        if step == 0:
            drain(landed.at[chunk, pl.ds(0, 3)], z_recv.at[chunk, q])
            drain(landed.at[chunk, 0], here_z.at[chunk])
        else:
            drain(landed.at[chunk, zs], z_recv.at[chunk, q])
        for d in range(1, 4):
            tx, ty = turn(x, d, X), turn(y, d, Y)
            remote(landed.at[chunk, zs, tx], cols[chunk].at[x, hi, core, y, lo],
                   xa_send.at[chunk], xa_recv.at[chunk, step], xs[d - 1]).start()
            remote(landed.at[chunk, zs, ty], rows.at[chunk, x, hi, y, lo],
                   ya_send.at[chunk], ya_recv.at[chunk, step], ys[d - 1]).start()
        local(landed.at[chunk, zs, x], cols[chunk].at[x, hi, core, y, lo], here_x.at[chunk, step]).start()
        local(landed.at[chunk, zs, y], rows.at[chunk, x, hi, y, lo], here_y.at[chunk, step]).start()

    def to_planes(chunk, step):
        hi, lo = of_quad(turn(quad, step, 4))
        drain(cols[chunk].at[pl.ds(0, 3), hi, core, y, lo], xa_recv.at[chunk, step])
        drain(cols[chunk].at[0, hi, core, y, lo], here_x.at[chunk, step])
        for d in (1, 3, 2):
            part = cols[chunk].at[:, hi, core, y, lo]
            remote(part, part, yg_send.at[chunk], yg_recv.at[chunk, step], ys[d - 1]).start()
        drain(rows.at[chunk, x, hi, pl.ds(0, 3), lo], ya_recv.at[chunk, step])
        drain(rows.at[chunk, x, hi, 0, lo], here_y.at[chunk, step])
        for d in (1, 3, 2):
            part = rows.at[chunk, x, hi, :, lo]
            remote(part, part, xg_send.at[chunk], xg_recv.at[chunk, step], xs[d - 1]).start()

    def to_twin(chunk, step):
        hi, lo = of_quad(turn(quad, step, 4))
        drain(cols[chunk].at[:, hi, core, pl.ds(0, 3), lo], yg_recv.at[chunk, step])
        part = cols[chunk].at[:, hi, core, :, lo]
        remote(part, part, c_send.at[chunk], c_recv.at[chunk, step], twin).start()

    lanes = lax.broadcasted_iota(jnp.int32, (64, 128), 1)
    sign = jnp.where(lanes < 64, 1.0, -1.0).astype(jnp.float32)

    def whole(chunk, p):
        return cols[chunk][lax.div(p, 4), lax.rem(lax.div(p, 2), 2), lax.rem(p, 2)].reshape(512, 128)

    def cross(chunk):
        def block(n, carry):
            tx, th = turn(x, lax.div(n, 2), X), turn(z_hi, lax.rem(n, 2), 2)
            own = rows[chunk, tx, th].reshape(512, 128)
            p = tx * 4 + th * 2 + core
            picked = jnp.concatenate([whole(chunk, partners[r, p]) for r in range(4)], axis=1)
            both = lax.dot_general(own, picked, (((0,), (0,)), ((), ())),
                                   preferred_element_type=jnp.float32)
            found = []
            for r in range(4):
                at = both[:, 128 * r:128 * (r + 1)]
                part = at[:64] + sign * pltpu.roll(at[64:], 64, 1)
                found.append(part.reshape(8, 8, 128))
            first = pl.multiple_of((tx * 2 + th) * ZL, ZL)
            parts[chunk, pl.ds(first, ZL)] = jnp.concatenate(found, axis=1).astype(jnp.bfloat16)

            def send(low, carry):
                tl = turn(z_lo, low, ZL)
                remote(parts.at[chunk, first + tl], out.at[chunk, z * X + x], o_send.at[chunk],
                       o_recv.at[chunk], device(tx, y, th * ZL + tl, core)).start()
                return carry

            lax.fori_loop(jnp.where(n == 0, 1, 0), ZL, send, 0)
            return carry

        lax.fori_loop(0, 8, block, 0)
        local(parts.at[chunk, (x * 2 + z_hi) * ZL + z_lo], out.at[chunk, z * X + x], here_o.at[chunk]).start()

    for chunk in range(2):
        for at in range(len(STEPS) + 2):
            if at < 4:
                to_groups(chunk, STEPS[at])
            if 0 <= at - 1 < 4:
                to_planes(chunk, STEPS[at - 1])
            if 0 <= at - 2 < 4:
                to_twin(chunk, STEPS[at - 2])
        for step in STEPS:
            hi, lo = of_quad(turn(quad, step, 4))
            drain(rows.at[chunk, pl.ds(0, 3), hi, :, lo], xg_recv.at[chunk, step])
            drain(cols[chunk].at[:, hi, 1 - core, :, lo], c_recv.at[chunk, step])
        cross(chunk)

    for chunk in range(2):
        drain(out.at[chunk, pl.ds(0, 63)], o_recv.at[chunk])
        drain(out.at[chunk, 0], here_o.at[chunk])
        drain(spec.at[chunk, pl.ds(0, 15)], z_send.at[chunk])
        drain(landed.at[chunk, pl.ds(0, 12)], xa_send.at[chunk])
        drain(landed.at[chunk, pl.ds(0, 12)], ya_send.at[chunk])
        drain(rows.at[chunk, pl.ds(0, 3)], xg_send.at[chunk])
        drain(rows.at[chunk, pl.ds(0, 3)], yg_send.at[chunk])
        drain(rows.at[chunk], c_send.at[chunk])
        drain(parts.at[chunk, pl.ds(0, 63)], o_send.at[chunk])


def exchange(partners, spec):
    vmem = pl.BlockSpec(memory_space=pltpu.VMEM)
    dma = pltpu.SemaphoreType.DMA
    one, four = dma((2,)), dma((2, 4))
    return pl.pallas_call(
        exchange_kernel,
        out_shape=jax.ShapeDtypeStruct((2, Z * X, 32, 128), jnp.bfloat16),
        in_specs=[pl.BlockSpec(memory_space=pltpu.SMEM), vmem],
        out_specs=vmem,
        scratch_shapes=[
            pltpu.VMEM((2, Z, 4, 16, 128), jnp.bfloat16),
            pltpu.VMEM((2, X, 2, Y, ZL, 16, 128), jnp.bfloat16),
            pltpu.VMEM((X, 2, CORES, Y, ZL, 16, 128), jnp.bfloat16),
            pltpu.VMEM((X, 2, CORES, Y, ZL, 16, 128), jnp.bfloat16),
            pltpu.VMEM((2, 64, 32, 128), jnp.bfloat16),
        ] + [one, four] * 6 + [one, one, one, four, four, one],
        compiler_params=pltpu.CompilerParams(
            collective_id=0, has_side_effects=True, vmem_limit_bytes=40 << 20
        ),
        cost_estimate=pl.CostEstimate(flops=1 << 30, bytes_accessed=9 << 20, transcendentals=0),
    )(partners, spec)


def lag_kernel(got, table, out, spread):
    width = table.shape[-1]
    column = lax.rem(lax.broadcasted_iota(jnp.int32, (64, width), 1), 16)
    for row in range(16):
        keep = jnp.where(column == row, 1.0, 0.0).astype(jnp.bfloat16)
        for kind in range(4):
            spread[kind, pl.ds(64 * row, 64), :] = table[kind] * keep
    for half in range(2):
        real, imag = [], []
        for g in range(0, 4, 2):
            a = got[:, :, g, pl.ds(16 * half, 16), :].reshape(width, 128)
            b = got[:, :, g + 1, pl.ds(16 * half, 16), :].reshape(width, 128)
            real += [a[:, :64], b[:, :64]]
            imag += [a[:, 64:], b[:, 64:]]
        real, imag = jnp.concatenate(real, axis=1), jnp.concatenate(imag, axis=1)
        dot = partial(jnp.dot, preferred_element_type=jnp.float32)
        lagged = (dot(spread[0], real) + dot(spread[1], imag)) + (
            dot(spread[2], real) + dot(spread[3], imag))
        out[pl.ds(2 * half, 2)] = lagged.astype(jnp.bfloat16).reshape(2, 8, 64, 256)


def lag(got, windows):
    weights = lag_table(64) / windows
    weights = jnp.transpose(weights.reshape(64, Z, 2, 2), (3, 0, 2, 1)).reshape(2, 64, 32)
    high = weights.astype(jnp.bfloat16)
    low = (weights - high.astype(jnp.float32)).astype(jnp.bfloat16)
    table = jnp.repeat(jnp.concatenate([high, low]), 16, axis=2)
    vmem = pl.BlockSpec(memory_space=pltpu.VMEM)
    return pl.pallas_call(
        lag_kernel,
        out_shape=jax.ShapeDtypeStruct((4, 8, 64, 256), jnp.bfloat16),
        in_specs=[vmem, vmem],
        out_specs=vmem,
        scratch_shapes=[pltpu.VMEM((4, 1024, 512), jnp.bfloat16)],
        compiler_params=pltpu.CompilerParams(vmem_limit_bytes=40 << 20),
        cost_estimate=pl.CostEstimate(flops=1 << 31, bytes_accessed=3 << 20, transcendentals=0),
    )(got.reshape(2, Z, X, 32, 128), table)


def shards(raw, valid, partners):
    win_dev, samples, width = raw.shape
    whitened = whiten(raw, valid[:, 0], samples)
    spec = jnp.transpose(whitened.reshape(win_dev, Z, 2, 2, 4, 64), (2, 1, 4, 0, 3, 5))
    got = exchange(partners, spec.reshape(2, Z, 4, win_dev, 128))
    return lag(got, 512)


def solution(mesh):
    return jax.shard_map(
        shards,
        mesh=mesh,
        in_specs=(P("stack", None, "pair"), P("stack", "pair"), P()),
        out_specs=P(None, ("pair", "stack"), None, None),
        check_vma=False,
    )
```

```python
from functools import partial
import math

import jax
import jax.numpy as jnp
import ml_dtypes
import numpy as np
from jax import lax
from jax.experimental import pallas as pl
from jax.experimental.pallas import tpu as pltpu
from jax.sharding import PartitionSpec as P

epsilon = 1e-06
MESH = pl.DeviceIdType.MESH
X, Y, Z, ZL, CORES = 4, 4, 16, 8, 2
ORDER = (1, 15, 2, 14, 3, 13, 4, 12, 5, 11, 6, 10, 7, 9, 8)
STEPS = (0, 1, 3, 2)
PLAN = [(stage, chunk, step) for chunk in (0, 1) for stage in "gpt" for step in range(4)]
PLAN = PLAN[:12] + [("x", 0, 0)] + PLAN[12:] + [("x", 1, 0)]


def split(table):
    high = table.astype(ml_dtypes.bfloat16)
    low = (table - high.astype(np.float64)).astype(ml_dtypes.bfloat16)
    return np.stack([high, low])


def forward_table():
    freqs = 1 + 2 * np.arange(Z)[None, :, None] + np.arange(2)[:, None, None]
    phases = freqs * np.arange(64) % 64 * (2.0 * math.pi / 64)
    return split(np.stack([np.cos(phases), -np.sin(phases)])).reshape(128, 64)


def lag_table(windows):
    freqs = 1 + 2 * np.arange(Z)[None, :] + np.arange(2)[:, None]
    phases = (np.arange(64) - 32)[:, None, None] * freqs % 64 * (2.0 * math.pi / 64)
    weights = np.where(freqs == 32, 1.0, 2.0) / windows
    table = split(np.stack([weights * np.cos(phases), weights * np.sin(phases)]))
    return np.repeat(table.reshape(4, 64, 32), 16, axis=2)


def place():
    pair, stack = lax.axis_index("pair"), lax.axis_index("stack")
    core = lax.rem(pair, 2)
    z_hi = lax.rem(lax.div(pair, 2), 2)
    return lax.div(pair, 4), lax.div(stack, ZL), z_hi * ZL + lax.rem(stack, ZL), core


def device(x, y, z, core):
    return (x * 4 + lax.div(z, ZL) * 2 + core, y * ZL + lax.rem(z, ZL))


def turn(index, by, size):
    return lax.rem(index + by, size)


def remote(src, dst, send, recv, to):
    return pltpu.make_async_remote_copy(
        src_ref=src, dst_ref=dst, send_sem=send, recv_sem=recv, device_id=to, device_id_type=MESH
    )


def local(src, dst, sem):
    return pltpu.make_async_copy(src, dst, sem)


def drain(ref, sem):
    pltpu.make_async_copy(ref, ref, sem).wait()


def whiten(raw, valid, table, mixed, spec):
    lanes = lax.broadcasted_iota(jnp.int32, (32, 128), 1)
    for w in range(16):
        both = jnp.dot(table[...], raw[w], preferred_element_type=jnp.float32)
        spectra = both[:64] + both[64:]
        re, im = spectra[:32], spectra[32:]
        power = jnp.sum(re * re + im * im, axis=1, keepdims=True) * (1.0 / 256)
        gain = lax.rsqrt(power + epsilon) * valid[w, 0].astype(jnp.float32)
        re, im = re * gain, im * gain
        for half in range(2):
            a, b = re[:, 128 * half:128 * (half + 1)], im[:, 128 * half:128 * (half + 1)]
            mixed[pl.ds(32 * half + w, 32, stride=64), :] = jnp.where(lanes < 64, a, pltpu.roll(b, 64, 1))
            mixed[pl.ds(32 * half + 16 + w, 32, stride=64), :] = jnp.where(lanes < 64, pltpu.roll(a, 64, 1), b)
    spec[...] = mixed[...].reshape(2, Z, 4, 16, 128).astype(jnp.bfloat16)


def exchange_kernel(partners, valid, raw_hbm, table, out, raw, mixed, spec, landed, rows, cols_0, cols_1, parts, z_send, z_recv, xa_send, xa_recv,
                    ya_send, ya_recv, xg_send, xg_recv, yg_send, yg_recv, c_send, c_recv,
                    o_send, o_recv, here_z, here_x, here_y, here_o, fetched):
    x, y, z, core = place()
    cols = (cols_0, cols_1)
    z_hi, z_lo = lax.div(z, ZL), lax.rem(z, ZL)
    xs = [device(turn(x, d, X), y, z, core) for d in range(1, X)]
    ys = [device(x, turn(y, d, Y), z, core) for d in range(1, Y)]
    twin = device(x, y, z, 1 - core)

    fetch = local(raw_hbm, raw, fetched)
    fetch.start()
    barrier = pltpu.get_barrier_semaphore()

    def greet(n, carry):
        to = device(turn(x, lax.div(n, Z), X), y, turn(z, lax.rem(n, Z), Z), core)
        pl.semaphore_signal(barrier, inc=1, device_id=to, device_id_type=MESH)
        return carry

    lax.fori_loop(1, 64, greet, 0)
    for peer in ys + [twin]:
        pl.semaphore_signal(barrier, inc=1, device_id=peer, device_id_type=MESH)
    fetch.wait()
    whiten(raw, valid, table, mixed, spec)
    pl.semaphore_wait(barrier, 67)

    quad = lax.div(z, 4)
    for chunk in range(2):
        local(spec.at[chunk, z], landed.at[chunk, z], here_z.at[chunk]).start()
        for by in ORDER:
            to = turn(z, by, Z)
            remote(spec.at[chunk, to], landed.at[chunk, z], z_send.at[chunk],
                   z_recv.at[chunk, quad], device(x, y, to, core)).start()

    def of_quad(q):
        return lax.div(q, 2), pl.ds(lax.rem(q, 2) * 4, 4)

    def to_groups(chunk, step):
        q = turn(quad, step, 4)
        hi, lo = of_quad(q)
        zs = pl.ds(q * 4, 4)
        if step == 0:
            drain(landed.at[chunk, pl.ds(0, 3)], z_recv.at[chunk, q])
            drain(landed.at[chunk, 0], here_z.at[chunk])
        else:
            drain(landed.at[chunk, zs], z_recv.at[chunk, q])
        for d in range(1, 4):
            tx, ty = turn(x, d, X), turn(y, d, Y)
            remote(landed.at[chunk, zs, tx], cols[chunk].at[x, hi, core, y, lo],
                   xa_send.at[chunk], xa_recv.at[chunk, step], xs[d - 1]).start()
            remote(landed.at[chunk, zs, ty], rows.at[chunk, x, hi, y, lo],
                   ya_send.at[chunk], ya_recv.at[chunk, step], ys[d - 1]).start()
        local(landed.at[chunk, zs, x], cols[chunk].at[x, hi, core, y, lo], here_x.at[chunk, step]).start()
        local(landed.at[chunk, zs, y], rows.at[chunk, x, hi, y, lo], here_y.at[chunk, step]).start()

    def to_planes(chunk, step):
        hi, lo = of_quad(turn(quad, step, 4))
        drain(cols[chunk].at[pl.ds(0, 3), hi, core, y, lo], xa_recv.at[chunk, step])
        drain(cols[chunk].at[0, hi, core, y, lo], here_x.at[chunk, step])
        for d in (1, 3, 2):
            part = cols[chunk].at[:, hi, core, y, lo]
            remote(part, part, yg_send.at[chunk], yg_recv.at[chunk, step], ys[d - 1]).start()
        drain(rows.at[chunk, x, hi, pl.ds(0, 3), lo], ya_recv.at[chunk, step])
        drain(rows.at[chunk, x, hi, 0, lo], here_y.at[chunk, step])
        for d in (1, 3, 2):
            part = rows.at[chunk, x, hi, :, lo]
            remote(part, part, xg_send.at[chunk], xg_recv.at[chunk, step], xs[d - 1]).start()

    def to_twin(chunk, step):
        hi, lo = of_quad(turn(quad, step, 4))
        drain(cols[chunk].at[:, hi, core, pl.ds(0, 3), lo], yg_recv.at[chunk, step])
        part = cols[chunk].at[:, hi, core, :, lo]
        remote(part, part, c_send.at[chunk], c_recv.at[chunk, step], twin).start()

    lanes = lax.broadcasted_iota(jnp.int32, (64, 128), 1)
    sign = jnp.where(lanes < 64, 1.0, -1.0).astype(jnp.float32)

    def whole(chunk, p):
        return cols[chunk][lax.div(p, 4), lax.rem(lax.div(p, 2), 2), lax.rem(p, 2)].reshape(512, 128)

    def block(chunk, tx, th):
        own = rows[chunk, tx, th].reshape(512, 128)
        p = tx * 4 + th * 2 + core
        picked = jnp.concatenate([whole(chunk, partners[r, p]) for r in range(4)], axis=1)
        both = lax.dot_general(own, picked, (((0,), (0,)), ((), ())),
                               preferred_element_type=jnp.float32)
        found = []
        for r in range(4):
            at = both[:, 128 * r:128 * (r + 1)]
            part = at[:64] + sign * pltpu.roll(at[64:], 64, 1)
            found.append(part.reshape(8, 8, 128))
        first = pl.multiple_of((tx * 2 + th) * ZL, ZL)
        parts[chunk, pl.ds(first, ZL)] = jnp.concatenate(found, axis=1).astype(jnp.bfloat16)

    def cross(chunk):
        def blocks(d, carry):
            tx = turn(x, d, X)
            block(chunk, tx, 0)
            block(chunk, tx, 1)

            def send(by):
                tz = turn(z, by, Z)
                remote(parts.at[chunk, tx * Z + tz], out.at[chunk, z * X + x], o_send.at[chunk],
                       o_recv.at[chunk], device(tx, y, tz, core)).start()

            for by in ORDER:
                send(by)
            pl.when(d > 0)(lambda: send(0))
            return carry

        lax.fori_loop(0, X, blocks, 0)
        local(parts.at[chunk, x * Z + z], out.at[chunk, z * X + x], here_o.at[chunk]).start()

    def ready(chunk):
        for step in STEPS:
            hi, lo = of_quad(turn(quad, step, 4))
            drain(rows.at[chunk, pl.ds(0, 3), hi, :, lo], xg_recv.at[chunk, step])
            drain(cols[chunk].at[:, hi, 1 - core, :, lo], c_recv.at[chunk, step])

    work = {"g": to_groups, "p": to_planes, "t": to_twin}
    for stage, chunk, step in PLAN:
        if stage == "x":
            ready(chunk)
            cross(chunk)
        else:
            work[stage](chunk, STEPS[step])

    for chunk in range(2):
        drain(out.at[chunk, pl.ds(0, 63)], o_recv.at[chunk])
        drain(out.at[chunk, 0], here_o.at[chunk])
        drain(spec.at[chunk, pl.ds(0, 15)], z_send.at[chunk])
        drain(landed.at[chunk, pl.ds(0, 12)], xa_send.at[chunk])
        drain(landed.at[chunk, pl.ds(0, 12)], ya_send.at[chunk])
        drain(rows.at[chunk, pl.ds(0, 3)], xg_send.at[chunk])
        drain(rows.at[chunk, pl.ds(0, 3)], yg_send.at[chunk])
        drain(rows.at[chunk], c_send.at[chunk])
        drain(parts.at[chunk, pl.ds(0, 63)], o_send.at[chunk])


def exchange(raw, valid, partners):
    vmem, smem = pl.BlockSpec(memory_space=pltpu.VMEM), pl.BlockSpec(memory_space=pltpu.SMEM)
    dma = pltpu.SemaphoreType.DMA
    one, four = dma((2,)), dma((2, 4))
    return pl.pallas_call(
        exchange_kernel,
        out_shape=jax.ShapeDtypeStruct((2, Z * X, 32, 128), jnp.bfloat16),
        in_specs=[smem, smem, pl.BlockSpec(memory_space=pl.ANY), vmem],
        out_specs=vmem,
        scratch_shapes=[
            pltpu.VMEM((16, 64, 256), jnp.bfloat16),
            pltpu.VMEM((2048, 128), jnp.float32),
            pltpu.VMEM((2, Z, 4, 16, 128), jnp.bfloat16),
            pltpu.VMEM((2, Z, 4, 16, 128), jnp.bfloat16),
            pltpu.VMEM((2, X, 2, Y, ZL, 16, 128), jnp.bfloat16),
            pltpu.VMEM((X, 2, CORES, Y, ZL, 16, 128), jnp.bfloat16),
            pltpu.VMEM((X, 2, CORES, Y, ZL, 16, 128), jnp.bfloat16),
            pltpu.VMEM((2, 64, 32, 128), jnp.bfloat16),
        ] + [one, four] * 6 + [one, one, one, four, four, one, dma],
        compiler_params=pltpu.CompilerParams(
            collective_id=0, has_side_effects=True, vmem_limit_bytes=40 << 20
        ),
        cost_estimate=pl.CostEstimate(flops=1 << 30, bytes_accessed=9 << 20, transcendentals=0),
    )(partners, valid, raw, jnp.asarray(forward_table()))


def lag_kernel(got, table, out, spread):
    width = table.shape[-1]
    column = lax.rem(lax.broadcasted_iota(jnp.int32, (64, width), 1), 16)
    for row in range(16):
        keep = jnp.where(column == row, 1.0, 0.0).astype(jnp.bfloat16)
        for kind in range(4):
            spread[kind, pl.ds(64 * row, 64), :] = table[kind] * keep
    for half in range(2):
        real, imag = [], []
        for g in range(0, 4, 2):
            a = got[:, :, g, pl.ds(16 * half, 16), :].reshape(width, 128)
            b = got[:, :, g + 1, pl.ds(16 * half, 16), :].reshape(width, 128)
            real += [a[:, :64], b[:, :64]]
            imag += [a[:, 64:], b[:, 64:]]
        real, imag = jnp.concatenate(real, axis=1), jnp.concatenate(imag, axis=1)
        dot = partial(jnp.dot, preferred_element_type=jnp.float32)
        lagged = (dot(spread[0], real) + dot(spread[1], imag)) + (
            dot(spread[2], real) + dot(spread[3], imag))
        out[pl.ds(2 * half, 2)] = lagged.astype(jnp.bfloat16).reshape(2, 8, 64, 256)


def lag(got, windows):
    vmem = pl.BlockSpec(memory_space=pltpu.VMEM)
    return pl.pallas_call(
        lag_kernel,
        out_shape=jax.ShapeDtypeStruct((4, 8, 64, 256), jnp.bfloat16),
        in_specs=[vmem, vmem],
        out_specs=vmem,
        scratch_shapes=[pltpu.VMEM((4, 1024, 512), jnp.bfloat16)],
        compiler_params=pltpu.CompilerParams(vmem_limit_bytes=40 << 20),
        cost_estimate=pl.CostEstimate(flops=1 << 31, bytes_accessed=3 << 20, transcendentals=0),
    )(got.reshape(2, Z, X, 32, 128), jnp.asarray(lag_table(windows)))


def shards(raw, valid, partners):
    return lag(exchange(raw, valid, partners), 512)


def solution(mesh):
    return jax.shard_map(
        shards,
        mesh=mesh,
        in_specs=(P("stack", None, "pair"), P("stack", "pair"), P()),
        out_specs=P(None, ("pair", "stack"), None, None),
        check_vma=False,
    )
```

```python
from functools import partial
import math

import jax
import jax.numpy as jnp
import ml_dtypes
import numpy as np
from jax import lax
from jax.experimental import pallas as pl
from jax.experimental.pallas import tpu as pltpu
from jax.sharding import PartitionSpec as P

epsilon = 1e-06
MESH = pl.DeviceIdType.MESH
X, Y, Z, ZL, CORES = 4, 4, 16, 8, 2
ORDER = (1, 15, 2, 14, 3, 13, 4, 12, 5, 11, 6, 10, 7, 9, 8)
STEPS = (0, 1, 3, 2)
PLAN = [(stage, chunk, step) for chunk in (0, 1) for stage in "gpt" for step in range(4)]
PLAN = PLAN[:12] + [("x", 0, 0)] + PLAN[12:] + [("x", 1, 0)]


def split(table):
    high = table.astype(ml_dtypes.bfloat16)
    low = (table - high.astype(np.float64)).astype(ml_dtypes.bfloat16)
    return np.stack([high, low])


def forward_table():
    freqs = 1 + 2 * np.arange(Z)[None, :, None] + np.arange(2)[:, None, None]
    phases = freqs * np.arange(64) % 64 * (2.0 * math.pi / 64)
    return split(np.stack([np.cos(phases), -np.sin(phases)])).reshape(128, 64)


def lag_table(windows):
    freqs = 1 + 2 * np.arange(Z)[None, :] + np.arange(2)[:, None]
    phases = (np.arange(64) - 32)[:, None, None] * freqs % 64 * (2.0 * math.pi / 64)
    weights = np.where(freqs == 32, 1.0, 2.0) / windows
    table = split(np.stack([weights * np.cos(phases), weights * np.sin(phases)]))
    return np.repeat(table.reshape(4, 64, 32), 16, axis=2)


def place():
    pair, stack = lax.axis_index("pair"), lax.axis_index("stack")
    core = lax.rem(pair, 2)
    z_hi = lax.rem(lax.div(pair, 2), 2)
    return lax.div(pair, 4), lax.div(stack, ZL), z_hi * ZL + lax.rem(stack, ZL), core


def device(x, y, z, core):
    return (x * 4 + lax.div(z, ZL) * 2 + core, y * ZL + lax.rem(z, ZL))


def turn(index, by, size):
    return lax.rem(index + by, size)


def remote(src, dst, send, recv, to):
    return pltpu.make_async_remote_copy(
        src_ref=src, dst_ref=dst, send_sem=send, recv_sem=recv, device_id=to, device_id_type=MESH
    )


def local(src, dst, sem):
    return pltpu.make_async_copy(src, dst, sem)


def drain(ref, sem):
    pltpu.make_async_copy(ref, ref, sem).wait()


def whiten(raw, valid, tables, mixed, spec):
    table = tables[4, :, :128].astype(jnp.bfloat16)
    table = jnp.concatenate([table[:, :64], table[:, 64:]], axis=0)
    lanes = lax.broadcasted_iota(jnp.int32, (32, 128), 1)
    for w in range(16):
        both = jnp.dot(table, raw[w], preferred_element_type=jnp.float32)
        spectra = both[:64] + both[64:]
        re, im = spectra[:32], spectra[32:]
        power = jnp.sum(re * re + im * im, axis=1, keepdims=True) * (1.0 / 256)
        gain = lax.rsqrt(power + epsilon) * valid[0, w].astype(jnp.float32)
        re, im = re * gain, im * gain
        for half in range(2):
            a, b = re[:, 128 * half:128 * (half + 1)], im[:, 128 * half:128 * (half + 1)]
            mixed[pl.ds(32 * half + w, 32, stride=64), :] = jnp.where(lanes < 64, a, pltpu.roll(b, 64, 1))
            mixed[pl.ds(32 * half + 16 + w, 32, stride=64), :] = jnp.where(lanes < 64, pltpu.roll(a, 64, 1), b)
    spec[...] = mixed[...].reshape(2, Z, 4, 16, 128).astype(jnp.bfloat16)


def spread_table(tables, chunk, spread):
    column = lax.rem(lax.broadcasted_iota(jnp.int32, (64, 256), 1), 16)
    for row in range(16):
        keep = jnp.where(column == row, 1.0, 0.0).astype(jnp.bfloat16)
        for kind in range(4):
            spread[kind, pl.ds(64 * row, 64), :] = tables[kind, :, 256 * chunk:256 * (chunk + 1)].astype(jnp.bfloat16) * keep


def lag_sum(got, spread, half):
    def rows(g):
        groups = [got[z * X + g, pl.ds(16 * half, 16), :] for z in range(Z)]
        return jnp.concatenate(groups, axis=0)

    groups = [rows(g) for g in range(4)]
    real = jnp.concatenate([g[:, :64] for g in groups], axis=1)
    imag = jnp.concatenate([g[:, 64:] for g in groups], axis=1)
    dot = partial(jnp.dot, preferred_element_type=jnp.float32)
    return (dot(spread[0], real) + dot(spread[1], imag)) + (dot(spread[2], real) + dot(spread[3], imag))


def kernel(partners_hbm, valid_hbm, raw_hbm, tables_hbm, out, partners, valid, tables,
                    got_0, got_1, spread_0, spread_1, lagged, result, raw, mixed,
                    spec, landed, rows, cols_0, cols_1, parts, z_send, z_recv, xa_send, xa_recv, ya_send,
                    ya_recv, xg_send, xg_recv, yg_send, yg_recv, c_send, c_recv, o_send, o_recv, here_z,
                    here_x, here_y, here_o, fetched, stored):
    x, y, z, core = place()
    cols, outs, spread = (cols_0, cols_1), (got_0, got_1), (spread_0, spread_1)
    z_hi, z_lo = lax.div(z, ZL), lax.rem(z, ZL)
    xs = [device(turn(x, d, X), y, z, core) for d in range(1, X)]
    ys = [device(x, turn(y, d, Y), z, core) for d in range(1, Y)]
    twin = device(x, y, z, 1 - core)

    fetches = [local(*pair, fetched.at[n]) for n, pair in enumerate(
        [(raw_hbm, raw), (tables_hbm, tables), (valid_hbm, valid), (partners_hbm, partners)])]
    for fetch in fetches:
        fetch.start()
    barrier = pltpu.get_barrier_semaphore()
    peers = [device(x, y, turn(z, by, Z), core) for by in range(1, Z)] + xs + ys + [twin]
    for peer in peers:
        pl.semaphore_signal(barrier, inc=1, device_id=peer, device_id_type=MESH)
    for fetch in fetches:
        fetch.wait()
    whiten(raw, valid, tables, mixed, spec)
    pl.semaphore_wait(barrier, len(peers))

    quad = lax.div(z, 4)
    for chunk in range(2):
        local(spec.at[chunk, z], landed.at[chunk, z], here_z.at[chunk]).start()
        for by in ORDER:
            to = turn(z, by, Z)
            remote(spec.at[chunk, to], landed.at[chunk, z], z_send.at[chunk],
                   z_recv.at[chunk, quad], device(x, y, to, core)).start()

    def of_quad(q):
        return lax.div(q, 2), pl.ds(lax.rem(q, 2) * 4, 4)

    def to_groups(chunk, step):
        q = turn(quad, step, 4)
        hi, lo = of_quad(q)
        zs = pl.ds(q * 4, 4)
        if step == 0:
            drain(landed.at[chunk, pl.ds(0, 3)], z_recv.at[chunk, q])
            drain(landed.at[chunk, 0], here_z.at[chunk])
        else:
            drain(landed.at[chunk, zs], z_recv.at[chunk, q])
        for d in range(1, 4):
            tx, ty = turn(x, d, X), turn(y, d, Y)
            remote(landed.at[chunk, zs, tx], cols[chunk].at[x, hi, core, y, lo],
                   xa_send.at[chunk], xa_recv.at[chunk, step], xs[d - 1]).start()
            remote(landed.at[chunk, zs, ty], rows.at[chunk, x, hi, y, lo],
                   ya_send.at[chunk], ya_recv.at[chunk, step], ys[d - 1]).start()
        local(landed.at[chunk, zs, x], cols[chunk].at[x, hi, core, y, lo], here_x.at[chunk, step]).start()
        local(landed.at[chunk, zs, y], rows.at[chunk, x, hi, y, lo], here_y.at[chunk, step]).start()

    def to_planes(chunk, step):
        hi, lo = of_quad(turn(quad, step, 4))
        drain(cols[chunk].at[pl.ds(0, 3), hi, core, y, lo], xa_recv.at[chunk, step])
        drain(cols[chunk].at[0, hi, core, y, lo], here_x.at[chunk, step])
        part = cols[chunk].at[:, hi, core, y, lo]
        for d in (1, 3, 2):
            remote(part, part, yg_send.at[chunk], yg_recv.at[chunk, step, d - 1], ys[d - 1]).start()
        remote(part, part, c_send.at[chunk], c_recv.at[chunk, step], twin).start()
        drain(rows.at[chunk, x, hi, pl.ds(0, 3), lo], ya_recv.at[chunk, step])
        drain(rows.at[chunk, x, hi, 0, lo], here_y.at[chunk, step])
        for d in (1, 3, 2):
            part = rows.at[chunk, x, hi, :, lo]
            remote(part, part, xg_send.at[chunk], xg_recv.at[chunk, step], xs[d - 1]).start()

    def to_twin(chunk, step):
        hi, lo = of_quad(turn(quad, step, 4))
        for d in (1, 3, 2):
            part = cols[chunk].at[:, hi, core, turn(y, 4 - d, Y), lo]
            drain(part, yg_recv.at[chunk, step, d - 1])
            remote(part, part, c_send.at[chunk], c_recv.at[chunk, step], twin).start()

    lanes = lax.broadcasted_iota(jnp.int32, (64, 128), 1)
    sign = jnp.where(lanes < 64, 1.0, -1.0).astype(jnp.float32)

    def whole(chunk, p):
        return cols[chunk][lax.div(p, 4), lax.rem(lax.div(p, 2), 2), lax.rem(p, 2)].reshape(512, 128)

    def block(chunk, tx, th):
        own = rows[chunk, tx, th].reshape(512, 128)
        p = tx * 4 + th * 2 + core
        picked = jnp.concatenate([whole(chunk, partners[r, p]) for r in range(4)], axis=1)
        both = lax.dot_general(own, picked, (((0,), (0,)), ((), ())),
                               preferred_element_type=jnp.float32)
        found = []
        for r in range(4):
            at = both[:, 128 * r:128 * (r + 1)]
            part = at[:64] + sign * pltpu.roll(at[64:], 64, 1)
            found.append(part.reshape(8, 8, 128))
        first = pl.multiple_of((tx * 2 + th) * ZL, ZL)
        parts[chunk, pl.ds(first, ZL)] = jnp.concatenate(found, axis=1).astype(jnp.bfloat16)

    def cross(chunk):
        def blocks(d, carry):
            tx = turn(x, d, X)
            block(chunk, tx, 0)
            block(chunk, tx, 1)

            def send(by):
                tz = turn(z, by, Z)
                remote(parts.at[chunk, tx * Z + tz], outs[chunk].at[z * X + x], o_send.at[chunk],
                       o_recv.at[chunk], device(tx, y, tz, core)).start()

            for by in ORDER:
                send(by)
            pl.when(d > 0)(lambda: send(0))
            return carry

        lax.fori_loop(0, X, blocks, 0)
        local(parts.at[chunk, x * Z + z], outs[chunk].at[z * X + x], here_o.at[chunk]).start()

    def ready(chunk):
        for step in STEPS:
            hi, lo = of_quad(turn(quad, step, 4))
            drain(rows.at[chunk, pl.ds(0, 3), hi, :, lo], xg_recv.at[chunk, step])
            drain(cols[chunk].at[:, hi, 1 - core, :, lo], c_recv.at[chunk, step])

    work = {"g": to_groups, "p": to_planes, "t": to_twin}
    for stage, chunk, step in PLAN:
        if stage == "x":
            ready(chunk)
            cross(chunk)
        else:
            work[stage](chunk, STEPS[step])

    for chunk in range(2):
        spread_table(tables, chunk, spread[chunk])
    for chunk in range(2):
        drain(outs[chunk].at[pl.ds(0, 63)], o_recv.at[chunk])
        drain(outs[chunk].at[0], here_o.at[chunk])
        for half in range(2):
            if chunk == 0:
                lagged[half] = lag_sum(got_0, spread_0, half)
            else:
                total = lagged[half] + lag_sum(got_1, spread_1, half)
                result[pl.ds(2 * half, 2)] = total.astype(jnp.bfloat16).reshape(2, 8, 64, 256)
                local(result.at[pl.ds(2 * half, 2)], out.at[pl.ds(2 * half, 2)], stored.at[half]).start()
        drain(spec.at[chunk, pl.ds(0, 15)], z_send.at[chunk])
        drain(landed.at[chunk, pl.ds(0, 12)], xa_send.at[chunk])
        drain(landed.at[chunk, pl.ds(0, 12)], ya_send.at[chunk])
        drain(rows.at[chunk, pl.ds(0, 3)], xg_send.at[chunk])
        drain(rows.at[chunk, pl.ds(0, 3)], yg_send.at[chunk])
        drain(rows.at[chunk], c_send.at[chunk])
        drain(parts.at[chunk, pl.ds(0, 63)], o_send.at[chunk])
    for half in range(2):
        drain(result.at[pl.ds(2 * half, 2)], stored.at[half])


def exchange(raw, valid, partners, tables):
    hbm = pl.BlockSpec(memory_space=pltpu.HBM)
    dma = pltpu.SemaphoreType.DMA
    one, four = dma((2,)), dma((2, 4))
    return pl.pallas_call(
        kernel,
        out_shape=jax.ShapeDtypeStruct((4, 8, 64, 256), jnp.bfloat16),
        in_specs=[hbm] * 4,
        out_specs=hbm,
        scratch_shapes=[
            pltpu.SMEM((4, 16), jnp.int32),
            pltpu.SMEM((1, 16), jnp.int32),
            pltpu.VMEM((5, 64, 512), jnp.float32),
            pltpu.VMEM((Z * X, 32, 128), jnp.bfloat16),
            pltpu.VMEM((Z * X, 32, 128), jnp.bfloat16),
            pltpu.VMEM((4, 1024, 256), jnp.bfloat16),
            pltpu.VMEM((4, 1024, 256), jnp.bfloat16),
            pltpu.VMEM((2, 1024, 256), jnp.float32),
            pltpu.VMEM((4, 8, 64, 256), jnp.bfloat16),
            pltpu.VMEM((16, 64, 256), jnp.bfloat16),
            pltpu.VMEM((2048, 128), jnp.float32),
            pltpu.VMEM((2, Z, 4, 16, 128), jnp.bfloat16),
            pltpu.VMEM((2, Z, 4, 16, 128), jnp.bfloat16),
            pltpu.VMEM((2, X, 2, Y, ZL, 16, 128), jnp.bfloat16),
            pltpu.VMEM((X, 2, CORES, Y, ZL, 16, 128), jnp.bfloat16),
            pltpu.VMEM((X, 2, CORES, Y, ZL, 16, 128), jnp.bfloat16),
            pltpu.VMEM((2, 64, 32, 128), jnp.bfloat16),
        ] + [one, four] * 4 + [one, dma((2, 4, 3)), one, four] + [one, one, one, four, four, one, dma((4,)), one],
        compiler_params=pltpu.CompilerParams(
            collective_id=0, has_side_effects=True, vmem_limit_bytes=62 << 20
        ),
        cost_estimate=pl.CostEstimate(flops=1 << 30, bytes_accessed=9 << 20, transcendentals=0),
    )(partners, valid.T, raw, tables)


def shards(raw, valid, partners):
    tables = np.zeros((5, 64, 512), np.float32)
    tables[:4] = lag_table(512)
    tables[4, :, :128] = np.concatenate(np.split(forward_table(), 2), axis=1)
    tables = jnp.asarray(tables)
    return exchange(raw, valid, partners, tables)


def solution(mesh):
    return jax.shard_map(
        shards,
        mesh=mesh,
        in_specs=(P("stack", None, "pair"), P("stack", "pair"), P()),
        out_specs=P(None, ("pair", "stack"), None, None),
        check_vma=False,
    )
```

```python
from functools import partial
import math

import jax
import jax.numpy as jnp
import ml_dtypes
import numpy as np
from jax import lax
from jax.experimental import pallas as pl
from jax.experimental.pallas import tpu as pltpu
from jax.sharding import PartitionSpec as P

epsilon = 1e-06
MESH = pl.DeviceIdType.MESH
X, Y, Z, ZL, CORES = 4, 4, 16, 8, 2
ORDER = (1, 15, 2, 14, 3, 13, 4, 12, 5, 11, 6, 10, 7, 9, 8)
PIECES = 4
STEPS = {4: (0, 1, 3, 2), 2: (0, 1), 1: (0,)}[PIECES]
DEPTH = Z // PIECES
PLAN = [(stage, chunk) for chunk in (0, 1) for stage in "gptx"]


def split(table):
    high = table.astype(ml_dtypes.bfloat16)
    low = (table - high.astype(np.float64)).astype(ml_dtypes.bfloat16)
    return np.stack([high, low])


def forward_table():
    freqs = 1 + 2 * np.arange(Z)[None, :, None] + np.arange(2)[:, None, None]
    phases = freqs * np.arange(64) % 64 * (2.0 * math.pi / 64)
    return split(np.stack([np.cos(phases), -np.sin(phases)])).reshape(128, 64)


def lag_table(windows):
    freqs = 1 + 2 * np.arange(Z)[None, :] + np.arange(2)[:, None]
    phases = (np.arange(64) - 32)[:, None, None] * freqs % 64 * (2.0 * math.pi / 64)
    weights = np.where(freqs == 32, 1.0, 2.0) / windows
    table = split(np.stack([weights * np.cos(phases), weights * np.sin(phases)]))
    return np.repeat(table.reshape(4, 64, 32), 16, axis=2)


def place():
    pair, stack = lax.axis_index("pair"), lax.axis_index("stack")
    core = lax.rem(pair, 2)
    z_hi = lax.rem(lax.div(pair, 2), 2)
    return lax.div(pair, 4), lax.div(stack, ZL), z_hi * ZL + lax.rem(stack, ZL), core


def device(x, y, z, core):
    return (x * 4 + lax.div(z, ZL) * 2 + core, y * ZL + lax.rem(z, ZL))


def turn(index, by, size):
    return lax.rem(index + by, size)


def remote(src, dst, send, recv, to):
    return pltpu.make_async_remote_copy(
        src_ref=src, dst_ref=dst, send_sem=send, recv_sem=recv, device_id=to, device_id_type=MESH
    )


def local(src, dst, sem):
    return pltpu.make_async_copy(src, dst, sem)


def drain(ref, sem):
    pltpu.make_async_copy(ref, ref, sem).wait()


def whiten(raw, valid, tables, mixed, spec):
    table = tables[4, :, :128].astype(jnp.bfloat16)
    table = jnp.concatenate([table[:, :64], table[:, 64:]], axis=0)
    lanes = lax.broadcasted_iota(jnp.int32, (32, 128), 1)
    for w in range(16):
        both = jnp.dot(table, raw[w], preferred_element_type=jnp.float32)
        spectra = both[:64] + both[64:]
        re, im = spectra[:32], spectra[32:]
        power = jnp.sum(re * re + im * im, axis=1, keepdims=True) * (1.0 / 256)
        gain = lax.rsqrt(power + epsilon) * valid[0, w].astype(jnp.float32)
        re, im = re * gain, im * gain
        for half in range(2):
            a, b = re[:, 128 * half:128 * (half + 1)], im[:, 128 * half:128 * (half + 1)]
            mixed[pl.ds(32 * half + w, 32, stride=64), :] = jnp.where(lanes < 64, a, pltpu.roll(b, 64, 1))
            mixed[pl.ds(32 * half + 16 + w, 32, stride=64), :] = jnp.where(lanes < 64, pltpu.roll(a, 64, 1), b)
    spec[...] = mixed[...].reshape(2, Z, 4, 16, 128).astype(jnp.bfloat16)


def spread_table(tables, chunk, spread):
    column = lax.rem(lax.broadcasted_iota(jnp.int32, (64, 256), 1), 16)
    for row in range(16):
        keep = jnp.where(column == row, 1.0, 0.0).astype(jnp.bfloat16)
        for kind in range(4):
            spread[kind, pl.ds(64 * row, 64), :] = tables[kind, :, 256 * chunk:256 * (chunk + 1)].astype(jnp.bfloat16) * keep


def lag_sum(got, spread, half):
    def rows(g):
        groups = [got[z * X + g, pl.ds(16 * half, 16), :] for z in range(Z)]
        return jnp.concatenate(groups, axis=0)

    groups = [rows(g) for g in range(4)]
    real = jnp.concatenate([g[:, :64] for g in groups], axis=1)
    imag = jnp.concatenate([g[:, 64:] for g in groups], axis=1)
    dot = partial(jnp.dot, preferred_element_type=jnp.float32)
    return (dot(spread[0], real) + dot(spread[1], imag)) + (dot(spread[2], real) + dot(spread[3], imag))


def kernel(partners_hbm, valid_hbm, raw_hbm, tables_hbm, out, partners, valid, tables,
                    got_0, got_1, spread_0, spread_1, lagged, result, raw, mixed,
                    spec, landed, rows, cols_0, cols_1, parts, z_send, z_recv, xa_send, xa_recv, ya_send,
                    ya_recv, xg_send, xg_recv, yg_send, yg_recv, c_send, c_recv, o_send, o_recv, here_z,
                    here_x, here_y, here_o, fetched, stored):
    x, y, z, core = place()
    cols, outs, spread = (cols_0, cols_1), (got_0, got_1), (spread_0, spread_1)
    z_hi, z_lo = lax.div(z, ZL), lax.rem(z, ZL)
    xs = [device(turn(x, d, X), y, z, core) for d in range(1, X)]
    ys = [device(x, turn(y, d, Y), z, core) for d in range(1, Y)]
    twin = device(x, y, z, 1 - core)

    fetches = [local(*pair, fetched.at[n]) for n, pair in enumerate(
        [(raw_hbm, raw), (tables_hbm, tables), (valid_hbm, valid), (partners_hbm, partners)])]
    for fetch in fetches:
        fetch.start()
    barrier = pltpu.get_barrier_semaphore()
    peers = [device(x, y, turn(z, by, Z), core) for by in range(1, Z)] + xs + ys + [twin]
    for peer in peers:
        pl.semaphore_signal(barrier, inc=1, device_id=peer, device_id_type=MESH)
    for fetch in fetches:
        fetch.wait()
    whiten(raw, valid, tables, mixed, spec)
    pl.semaphore_wait(barrier, len(peers))

    piece = lax.div(z, DEPTH)
    for chunk in range(2):
        local(spec.at[chunk, z], landed.at[chunk, z], here_z.at[chunk]).start()
        for by in ORDER:
            to = turn(z, by, Z)
            remote(spec.at[chunk, to], landed.at[chunk, z], z_send.at[chunk],
                   z_recv.at[chunk, piece], device(x, y, to, core)).start()

    def part_of(q):
        if PIECES == 1:
            return slice(None), slice(None)
        if PIECES == 2:
            return q, slice(None)
        return lax.div(q, 2), pl.ds(lax.rem(q, 2) * DEPTH, DEPTH)

    def to_groups(chunk, step):
        q = turn(piece, step, PIECES)
        hi, lo = part_of(q)
        zs = pl.ds(q * DEPTH, DEPTH)
        if step == 0:
            drain(landed.at[chunk, pl.ds(0, DEPTH - 1)], z_recv.at[chunk, q])
            drain(landed.at[chunk, 0], here_z.at[chunk])
        else:
            drain(landed.at[chunk, zs], z_recv.at[chunk, q])
        for d in range(1, 4):
            tx, ty = turn(x, d, X), turn(y, d, Y)
            remote(landed.at[chunk, zs, tx], cols[chunk].at[x, hi, core, y, lo],
                   xa_send.at[chunk], xa_recv.at[chunk, step], xs[d - 1]).start()
            remote(landed.at[chunk, zs, ty], rows.at[chunk, x, hi, y, lo],
                   ya_send.at[chunk], ya_recv.at[chunk, step], ys[d - 1]).start()
        local(landed.at[chunk, zs, x], cols[chunk].at[x, hi, core, y, lo], here_x.at[chunk, step]).start()
        local(landed.at[chunk, zs, y], rows.at[chunk, x, hi, y, lo], here_y.at[chunk, step]).start()

    def to_planes(chunk, step):
        hi, lo = part_of(turn(piece, step, PIECES))
        drain(cols[chunk].at[pl.ds(0, 3), hi, core, y, lo], xa_recv.at[chunk, step])
        drain(cols[chunk].at[0, hi, core, y, lo], here_x.at[chunk, step])
        part = cols[chunk].at[:, hi, core, y, lo]
        for d in (1, 3, 2):
            remote(part, part, yg_send.at[chunk], yg_recv.at[chunk, step, d - 1], ys[d - 1]).start()
        remote(part, part, c_send.at[chunk], c_recv.at[chunk, step], twin).start()
        drain(rows.at[chunk, x, hi, pl.ds(0, 3), lo], ya_recv.at[chunk, step])
        drain(rows.at[chunk, x, hi, 0, lo], here_y.at[chunk, step])
        for d in (1, 3, 2):
            part = rows.at[chunk, x, hi, :, lo]
            remote(part, part, xg_send.at[chunk], xg_recv.at[chunk, step], xs[d - 1]).start()

    def to_twin(chunk, step):
        hi, lo = part_of(turn(piece, step, PIECES))
        for d in (1, 3, 2):
            part = cols[chunk].at[:, hi, core, turn(y, 4 - d, Y), lo]
            drain(part, yg_recv.at[chunk, step, d - 1])
            remote(part, part, c_send.at[chunk], c_recv.at[chunk, step], twin).start()

    lanes = lax.broadcasted_iota(jnp.int32, (64, 128), 1)
    sign = jnp.where(lanes < 64, 1.0, -1.0).astype(jnp.float32)

    def whole(chunk, p):
        return cols[chunk][lax.div(p, 4), lax.rem(lax.div(p, 2), 2), lax.rem(p, 2)].reshape(512, 128)

    def block(chunk, tx, th):
        own = rows[chunk, tx, th].reshape(512, 128)
        p = tx * 4 + th * 2 + core
        picked = jnp.concatenate([whole(chunk, partners[r, p]) for r in range(4)], axis=1)
        both = lax.dot_general(own, picked, (((0,), (0,)), ((), ())),
                               preferred_element_type=jnp.float32)
        found = []
        for r in range(4):
            at = both[:, 128 * r:128 * (r + 1)]
            part = at[:64] + sign * pltpu.roll(at[64:], 64, 1)
            found.append(part.reshape(8, 8, 128))
        first = pl.multiple_of((tx * 2 + th) * ZL, ZL)
        parts[chunk, pl.ds(first, ZL)] = jnp.concatenate(found, axis=1).astype(jnp.bfloat16)

    def cross(chunk):
        def blocks(n, carry):
            tx = turn(x, 3 - n, X)
            block(chunk, tx, 0)
            block(chunk, tx, 1)

            def send(by):
                tz = turn(z, by, Z)
                remote(parts.at[chunk, tx * Z + tz], outs[chunk].at[z * X + x], o_send.at[chunk],
                       o_recv.at[chunk], device(tx, y, tz, core)).start()

            for by in ORDER[::-1]:
                send(by)
            pl.when(n < 3)(lambda: send(0))
            return carry

        lax.fori_loop(0, X, blocks, 0)
        local(parts.at[chunk, x * Z + z], outs[chunk].at[z * X + x], here_o.at[chunk]).start()

    def ready(chunk):
        for step in STEPS:
            hi, lo = part_of(turn(piece, step, PIECES))
            drain(rows.at[chunk, pl.ds(0, 3), hi, :, lo], xg_recv.at[chunk, step])
            drain(cols[chunk].at[:, hi, 1 - core, :, lo], c_recv.at[chunk, step])

    work = {"g": to_groups, "p": to_planes, "t": to_twin}
    for stage, chunk in PLAN:
        if stage == "x":
            ready(chunk)
            cross(chunk)
        else:
            for step in STEPS:
                work[stage](chunk, step)

    for chunk in range(2):
        spread_table(tables, chunk, spread[chunk])
    for chunk in range(2):
        drain(outs[chunk].at[pl.ds(0, 63)], o_recv.at[chunk])
        drain(outs[chunk].at[0], here_o.at[chunk])
        for half in range(2):
            if chunk == 0:
                lagged[half] = lag_sum(got_0, spread_0, half)
            else:
                total = lagged[half] + lag_sum(got_1, spread_1, half)
                result[pl.ds(2 * half, 2)] = total.astype(jnp.bfloat16).reshape(2, 8, 64, 256)
                local(result.at[pl.ds(2 * half, 2)], out.at[pl.ds(2 * half, 2)], stored.at[half]).start()
        drain(spec.at[chunk, pl.ds(0, 15)], z_send.at[chunk])
        drain(landed.at[chunk, pl.ds(0, 12)], xa_send.at[chunk])
        drain(landed.at[chunk, pl.ds(0, 12)], ya_send.at[chunk])
        drain(rows.at[chunk, pl.ds(0, 3)], xg_send.at[chunk])
        drain(rows.at[chunk, pl.ds(0, 3)], yg_send.at[chunk])
        drain(rows.at[chunk], c_send.at[chunk])
        drain(parts.at[chunk, pl.ds(0, 63)], o_send.at[chunk])
    for half in range(2):
        drain(result.at[pl.ds(2 * half, 2)], stored.at[half])


def exchange(raw, valid, partners, tables):
    hbm = pl.BlockSpec(memory_space=pltpu.HBM)
    dma = pltpu.SemaphoreType.DMA
    one, four = dma((2,)), dma((2, 4))
    return pl.pallas_call(
        kernel,
        out_shape=jax.ShapeDtypeStruct((4, 8, 64, 256), jnp.bfloat16),
        in_specs=[hbm] * 4,
        out_specs=hbm,
        scratch_shapes=[
            pltpu.SMEM((4, 16), jnp.int32),
            pltpu.SMEM((1, 16), jnp.int32),
            pltpu.VMEM((5, 64, 512), jnp.float32),
            pltpu.VMEM((Z * X, 32, 128), jnp.bfloat16),
            pltpu.VMEM((Z * X, 32, 128), jnp.bfloat16),
            pltpu.VMEM((4, 1024, 256), jnp.bfloat16),
            pltpu.VMEM((4, 1024, 256), jnp.bfloat16),
            pltpu.VMEM((2, 1024, 256), jnp.float32),
            pltpu.VMEM((4, 8, 64, 256), jnp.bfloat16),
            pltpu.VMEM((16, 64, 256), jnp.bfloat16),
            pltpu.VMEM((2048, 128), jnp.float32),
            pltpu.VMEM((2, Z, 4, 16, 128), jnp.bfloat16),
            pltpu.VMEM((2, Z, 4, 16, 128), jnp.bfloat16),
            pltpu.VMEM((2, X, 2, Y, ZL, 16, 128), jnp.bfloat16),
            pltpu.VMEM((X, 2, CORES, Y, ZL, 16, 128), jnp.bfloat16),
            pltpu.VMEM((X, 2, CORES, Y, ZL, 16, 128), jnp.bfloat16),
            pltpu.VMEM((2, 64, 32, 128), jnp.bfloat16),
        ] + [one, four] * 4 + [one, dma((2, 4, 3)), one, four] + [one, one, one, four, four, one, dma((4,)), one],
        compiler_params=pltpu.CompilerParams(
            collective_id=0, has_side_effects=True, vmem_limit_bytes=62 << 20
        ),
        cost_estimate=pl.CostEstimate(flops=1 << 30, bytes_accessed=9 << 20, transcendentals=0),
    )(partners, valid.T, raw, tables)


def shards(raw, valid, partners):
    tables = np.zeros((5, 64, 512), np.float32)
    tables[:4] = lag_table(512)
    tables[4, :, :128] = np.concatenate(np.split(forward_table(), 2), axis=1)
    tables = jnp.asarray(tables)
    return exchange(raw, valid, partners, tables)


def solution(mesh):
    return jax.shard_map(
        shards,
        mesh=mesh,
        in_specs=(P("stack", None, "pair"), P("stack", "pair"), P()),
        out_specs=P(None, ("pair", "stack"), None, None),
        check_vma=False,
    )
```

```python
from functools import partial
import math

import jax
import jax.numpy as jnp
import ml_dtypes
import numpy as np
from jax import lax
from jax.experimental import pallas as pl
from jax.experimental.pallas import tpu as pltpu
from jax.sharding import PartitionSpec as P

epsilon = 1e-06
MESH = pl.DeviceIdType.MESH
X, Y, Z, ZL, CORES = 4, 4, 16, 8, 2
ORDER = (1, 15, 2, 14, 3, 13, 4, 12, 5, 11, 6, 10, 7, 9, 8)
PIECES = 4
STEPS = {4: (0, 1, 3, 2), 2: (0, 1), 1: (0,)}[PIECES]
DEPTH = Z // PIECES
PLAN = [(stage, chunk) for chunk in (0, 1) for stage in "gptx"]


def split(table):
    high = table.astype(ml_dtypes.bfloat16)
    low = (table - high.astype(np.float64)).astype(ml_dtypes.bfloat16)
    return np.stack([high, low])


def forward_table():
    freqs = 1 + 2 * np.arange(Z)[None, :, None] + np.arange(2)[:, None, None]
    phases = freqs * np.arange(64) % 64 * (2.0 * math.pi / 64)
    return split(np.stack([np.cos(phases), -np.sin(phases)])).reshape(128, 64)


def lag_table(windows):
    freqs = 1 + 2 * np.arange(Z)[None, :] + np.arange(2)[:, None]
    phases = (np.arange(64) - 32)[:, None, None] * freqs % 64 * (2.0 * math.pi / 64)
    weights = np.where(freqs == 32, 1.0, 2.0) / windows
    table = split(np.stack([weights * np.cos(phases), weights * np.sin(phases)]))
    return np.repeat(table.reshape(4, 64, 32), 16, axis=2)


def place():
    pair, stack = lax.axis_index("pair"), lax.axis_index("stack")
    core = lax.rem(pair, 2)
    z_hi = lax.rem(lax.div(pair, 2), 2)
    return lax.div(pair, 4), lax.div(stack, ZL), z_hi * ZL + lax.rem(stack, ZL), core


def device(x, y, z, core):
    return (x * 4 + lax.div(z, ZL) * 2 + core, y * ZL + lax.rem(z, ZL))


def turn(index, by, size):
    return lax.rem(index + by, size)


def remote(src, dst, send, recv, to):
    return pltpu.make_async_remote_copy(
        src_ref=src, dst_ref=dst, send_sem=send, recv_sem=recv, device_id=to, device_id_type=MESH
    )


def local(src, dst, sem):
    return pltpu.make_async_copy(src, dst, sem)


def drain(ref, sem):
    pltpu.make_async_copy(ref, ref, sem).wait()


def whiten(raw, valid, tables, mixed, spec):
    table = tables[4, :, :128].astype(jnp.bfloat16)
    table = jnp.concatenate([table[:, :64], table[:, 64:]], axis=0)
    lanes = lax.broadcasted_iota(jnp.int32, (32, 128), 1)
    for w in range(16):
        both = jnp.dot(table, raw[w], preferred_element_type=jnp.float32)
        spectra = both[:64] + both[64:]
        re, im = spectra[:32], spectra[32:]
        power = jnp.sum(re * re + im * im, axis=1, keepdims=True) * (1.0 / 256)
        gain = lax.rsqrt(power + epsilon) * valid[0, w].astype(jnp.float32)
        re, im = re * gain, im * gain
        for half in range(2):
            a, b = re[:, 128 * half:128 * (half + 1)], im[:, 128 * half:128 * (half + 1)]
            mixed[pl.ds(32 * half + w, 32, stride=64), :] = jnp.where(lanes < 64, a, pltpu.roll(b, 64, 1))
            mixed[pl.ds(32 * half + 16 + w, 32, stride=64), :] = jnp.where(lanes < 64, pltpu.roll(a, 64, 1), b)
    spec[...] = mixed[...].reshape(2, Z, 4, 16, 128).astype(jnp.bfloat16)


def spread_table(tables, chunk, spread):
    column = lax.rem(lax.broadcasted_iota(jnp.int32, (64, 256), 1), 16)
    for row in range(16):
        keep = jnp.where(column == row, 1.0, 0.0).astype(jnp.bfloat16)
        for kind in range(4):
            spread[kind, pl.ds(64 * row, 64), :] = tables[kind, :, 256 * chunk:256 * (chunk + 1)].astype(jnp.bfloat16) * keep


def lag_sum(got, spread, half):
    def rows(g):
        groups = [got[z * X + g, pl.ds(16 * half, 16), :] for z in range(Z)]
        return jnp.concatenate(groups, axis=0)

    groups = [rows(g) for g in range(4)]
    real = jnp.concatenate([g[:, :64] for g in groups], axis=1)
    imag = jnp.concatenate([g[:, 64:] for g in groups], axis=1)
    dot = partial(jnp.dot, preferred_element_type=jnp.float32)
    return (dot(spread[0], real) + dot(spread[1], imag)) + (dot(spread[2], real) + dot(spread[3], imag))


def kernel(partners_hbm, valid_hbm, raw_hbm, tables_hbm, out, partners, valid, tables,
                    got_0, got_1, spread_0, spread_1, lagged, result, raw, mixed,
                    spec, landed, rows, cols_0, cols_1, parts, z_send, z_recv, xa_send, xa_recv, ya_send,
                    ya_recv, xg_send, xg_recv, yg_send, yg_recv, c_send, c_recv, o_send, o_recv, here_z,
                    here_x, here_y, here_o, fetched, stored):
    x, y, z, core = place()
    cols, outs, spread = (cols_0, cols_1), (got_0, got_1), (spread_0, spread_1)
    z_hi, z_lo = lax.div(z, ZL), lax.rem(z, ZL)
    xs = [device(turn(x, d, X), y, z, core) for d in range(1, X)]
    ys = [device(x, turn(y, d, Y), z, core) for d in range(1, Y)]
    twin = device(x, y, z, 1 - core)

    fetches = [local(*pair, fetched.at[n]) for n, pair in enumerate(
        [(raw_hbm, raw), (tables_hbm, tables), (valid_hbm, valid), (partners_hbm, partners)])]
    for fetch in fetches:
        fetch.start()
    barrier = pltpu.get_barrier_semaphore()
    peers = [device(x, y, turn(z, by, Z), core) for by in ORDER[::-1]] + xs + ys + [twin]
    for peer in peers:
        pl.semaphore_signal(barrier, inc=1, device_id=peer, device_id_type=MESH)
    for fetch in fetches:
        fetch.wait()
    whiten(raw, valid, tables, mixed, spec)
    pl.semaphore_wait(barrier, len(peers))

    piece = lax.div(z, DEPTH)
    for chunk in range(2):
        local(spec.at[chunk, z], landed.at[chunk, z], here_z.at[chunk]).start()
        for by in ORDER:
            to = turn(z, by, Z)
            remote(spec.at[chunk, to], landed.at[chunk, z], z_send.at[chunk],
                   z_recv.at[chunk, piece], device(x, y, to, core)).start()

    def part_of(q):
        if PIECES == 1:
            return slice(None), slice(None)
        if PIECES == 2:
            return q, slice(None)
        return lax.div(q, 2), pl.ds(lax.rem(q, 2) * DEPTH, DEPTH)

    def to_groups(chunk, step):
        q = turn(piece, step, PIECES)
        hi, lo = part_of(q)
        zs = pl.ds(q * DEPTH, DEPTH)
        if step == 0:
            drain(landed.at[chunk, pl.ds(0, DEPTH - 1)], z_recv.at[chunk, q])
            drain(landed.at[chunk, 0], here_z.at[chunk])
        else:
            drain(landed.at[chunk, zs], z_recv.at[chunk, q])
        for d in range(1, 4):
            tx, ty = turn(x, d, X), turn(y, d, Y)
            remote(landed.at[chunk, zs, tx], cols[chunk].at[x, hi, core, y, lo],
                   xa_send.at[chunk], xa_recv.at[chunk, step], xs[d - 1]).start()
            remote(landed.at[chunk, zs, ty], rows.at[chunk, x, hi, y, lo],
                   ya_send.at[chunk], ya_recv.at[chunk, step], ys[d - 1]).start()
        local(landed.at[chunk, zs, x], cols[chunk].at[x, hi, core, y, lo], here_x.at[chunk, step]).start()
        local(landed.at[chunk, zs, y], rows.at[chunk, x, hi, y, lo], here_y.at[chunk, step]).start()

    def to_planes(chunk, step):
        hi, lo = part_of(turn(piece, step, PIECES))
        drain(cols[chunk].at[pl.ds(0, 3), hi, core, y, lo], xa_recv.at[chunk, step])
        drain(cols[chunk].at[0, hi, core, y, lo], here_x.at[chunk, step])
        part = cols[chunk].at[:, hi, core, y, lo]
        for d in (1, 3, 2):
            remote(part, part, yg_send.at[chunk], yg_recv.at[chunk, step, d - 1], ys[d - 1]).start()
        remote(part, part, c_send.at[chunk], c_recv.at[chunk, step], twin).start()
        drain(rows.at[chunk, x, hi, pl.ds(0, 3), lo], ya_recv.at[chunk, step])
        drain(rows.at[chunk, x, hi, 0, lo], here_y.at[chunk, step])
        for d in (1, 3, 2):
            part = rows.at[chunk, x, hi, :, lo]
            remote(part, part, xg_send.at[chunk], xg_recv.at[chunk, step], xs[d - 1]).start()

    def to_twin(chunk, step):
        hi, lo = part_of(turn(piece, step, PIECES))
        for d in (1, 3, 2):
            part = cols[chunk].at[:, hi, core, turn(y, 4 - d, Y), lo]
            drain(part, yg_recv.at[chunk, step, d - 1])
            remote(part, part, c_send.at[chunk], c_recv.at[chunk, step], twin).start()

    lanes = lax.broadcasted_iota(jnp.int32, (64, 128), 1)
    sign = jnp.where(lanes < 64, 1.0, -1.0).astype(jnp.float32)

    def whole(chunk, p):
        return cols[chunk][lax.div(p, 4), lax.rem(lax.div(p, 2), 2), lax.rem(p, 2)].reshape(512, 128)

    def block(chunk, tx, th):
        own = rows[chunk, tx, th].reshape(512, 128)
        p = tx * 4 + th * 2 + core
        picked = jnp.concatenate([whole(chunk, partners[r, p]) for r in range(4)], axis=1)
        both = lax.dot_general(own, picked, (((0,), (0,)), ((), ())),
                               preferred_element_type=jnp.float32)
        found = []
        for r in range(4):
            at = both[:, 128 * r:128 * (r + 1)]
            part = at[:64] + sign * pltpu.roll(at[64:], 64, 1)
            found.append(part.reshape(8, 8, 128))
        first = pl.multiple_of((tx * 2 + th) * ZL, ZL)
        parts[chunk, pl.ds(first, ZL)] = jnp.concatenate(found, axis=1).astype(jnp.bfloat16)

    def cross(chunk):
        def blocks(n, carry):
            tx = turn(x, 3 - n, X)
            block(chunk, tx, 0)
            block(chunk, tx, 1)

            def send(by):
                tz = turn(z, by, Z)
                remote(parts.at[chunk, tx * Z + tz], outs[chunk].at[z * X + x], o_send.at[chunk],
                       o_recv.at[chunk], device(tx, y, tz, core)).start()

            for by in ORDER[::-1]:
                send(by)
            pl.when(n < 3)(lambda: send(0))
            return carry

        lax.fori_loop(0, X, blocks, 0)
        local(parts.at[chunk, x * Z + z], outs[chunk].at[z * X + x], here_o.at[chunk]).start()

    def ready(chunk):
        for step in STEPS:
            hi, lo = part_of(turn(piece, step, PIECES))
            drain(rows.at[chunk, pl.ds(0, 3), hi, :, lo], xg_recv.at[chunk, step])
            drain(cols[chunk].at[:, hi, 1 - core, :, lo], c_recv.at[chunk, step])

    work = {"g": to_groups, "p": to_planes, "t": to_twin}
    for stage, chunk in PLAN:
        if stage == "x":
            ready(chunk)
            cross(chunk)
        else:
            for step in STEPS:
                work[stage](chunk, step)

    for chunk in range(2):
        spread_table(tables, chunk, spread[chunk])
    for chunk in range(2):
        drain(outs[chunk].at[pl.ds(0, 63)], o_recv.at[chunk])
        drain(outs[chunk].at[0], here_o.at[chunk])
        for half in range(2):
            if chunk == 0:
                lagged[half] = lag_sum(got_0, spread_0, half)
            else:
                total = lagged[half] + lag_sum(got_1, spread_1, half)
                result[pl.ds(2 * half, 2)] = total.astype(jnp.bfloat16).reshape(2, 8, 64, 256)
                local(result.at[pl.ds(2 * half, 2)], out.at[pl.ds(2 * half, 2)], stored.at[half]).start()
        drain(spec.at[chunk, pl.ds(0, 15)], z_send.at[chunk])
        drain(landed.at[chunk, pl.ds(0, 12)], xa_send.at[chunk])
        drain(landed.at[chunk, pl.ds(0, 12)], ya_send.at[chunk])
        drain(rows.at[chunk, pl.ds(0, 3)], xg_send.at[chunk])
        drain(rows.at[chunk, pl.ds(0, 3)], yg_send.at[chunk])
        drain(rows.at[chunk], c_send.at[chunk])
        drain(parts.at[chunk, pl.ds(0, 63)], o_send.at[chunk])
    for half in range(2):
        drain(result.at[pl.ds(2 * half, 2)], stored.at[half])


def exchange(raw, valid, partners, tables):
    hbm = pl.BlockSpec(memory_space=pltpu.HBM)
    dma = pltpu.SemaphoreType.DMA
    one, four = dma((2,)), dma((2, 4))
    return pl.pallas_call(
        kernel,
        out_shape=jax.ShapeDtypeStruct((4, 8, 64, 256), jnp.bfloat16),
        in_specs=[hbm] * 4,
        out_specs=hbm,
        scratch_shapes=[
            pltpu.SMEM((4, 16), jnp.int32),
            pltpu.SMEM((1, 16), jnp.int32),
            pltpu.VMEM((5, 64, 512), jnp.float32),
            pltpu.VMEM((Z * X, 32, 128), jnp.bfloat16),
            pltpu.VMEM((Z * X, 32, 128), jnp.bfloat16),
            pltpu.VMEM((4, 1024, 256), jnp.bfloat16),
            pltpu.VMEM((4, 1024, 256), jnp.bfloat16),
            pltpu.VMEM((2, 1024, 256), jnp.float32),
            pltpu.VMEM((4, 8, 64, 256), jnp.bfloat16),
            pltpu.VMEM((16, 64, 256), jnp.bfloat16),
            pltpu.VMEM((2048, 128), jnp.float32),
            pltpu.VMEM((2, Z, 4, 16, 128), jnp.bfloat16),
            pltpu.VMEM((2, Z, 4, 16, 128), jnp.bfloat16),
            pltpu.VMEM((2, X, 2, Y, ZL, 16, 128), jnp.bfloat16),
            pltpu.VMEM((X, 2, CORES, Y, ZL, 16, 128), jnp.bfloat16),
            pltpu.VMEM((X, 2, CORES, Y, ZL, 16, 128), jnp.bfloat16),
            pltpu.VMEM((2, 64, 32, 128), jnp.bfloat16),
        ] + [one, four] * 4 + [one, dma((2, 4, 3)), one, four] + [one, one, one, four, four, one, dma((4,)), one],
        compiler_params=pltpu.CompilerParams(
            collective_id=0, has_side_effects=True, vmem_limit_bytes=62 << 20
        ),
        cost_estimate=pl.CostEstimate(flops=1 << 30, bytes_accessed=9 << 20, transcendentals=0),
    )(partners, valid.T, raw, tables)


def copy_kernel(src, out, held, sems):
    takes = [local(src.at[r], held.at[r], sems.at[r]) for r in range(4)]
    gives = [local(held.at[r], out.at[r], sems.at[r + 4]) for r in range(4)]
    for take in takes:
        take.start()
    for take, give in zip(takes, gives):
        take.wait()
        give.start()
    for give in gives:
        give.wait()


def hand_over(lagged):
    hbm = pl.BlockSpec(memory_space=pltpu.HBM)
    return pl.pallas_call(
        copy_kernel,
        out_shape=jax.ShapeDtypeStruct((4, 8, 64, 256), jnp.bfloat16),
        in_specs=[hbm],
        out_specs=hbm,
        scratch_shapes=[pltpu.VMEM((4, 8, 64, 256), jnp.bfloat16), pltpu.SemaphoreType.DMA((8,))],
        compiler_params=pltpu.CompilerParams(vmem_limit_bytes=62 << 20),
        cost_estimate=pl.CostEstimate(flops=0, bytes_accessed=2 << 20, transcendentals=0),
    )(lagged)


def shards(raw, valid, partners):
    tables = np.zeros((5, 64, 512), np.float32)
    tables[:4] = lag_table(512)
    tables[4, :, :128] = np.concatenate(np.split(forward_table(), 2), axis=1)
    tables = jnp.asarray(tables)
    return hand_over(exchange(raw, valid, partners, tables))


def solution(mesh):
    return jax.shard_map(
        shards,
        mesh=mesh,
        in_specs=(P("stack", None, "pair"), P("stack", "pair"), P()),
        out_specs=P(None, ("pair", "stack"), None, None),
        check_vma=False,
    )
```

```python
from functools import partial
import math

import jax
import jax.numpy as jnp
import ml_dtypes
import numpy as np
from jax import lax
from jax.experimental import pallas as pl
from jax.experimental.pallas import tpu as pltpu
from jax.sharding import PartitionSpec as P

epsilon = 1e-06
MESH = pl.DeviceIdType.MESH
X, Y, Z, ZL, CORES = 4, 4, 16, 8, 2
ORDER = (1, 15, 2, 14, 3, 13, 4, 12, 5, 11, 6, 10, 7, 9, 8)
PIECES = 4
STEPS = {4: (0, 1, 3, 2), 2: (0, 1), 1: (0,)}[PIECES]
DEPTH = Z // PIECES
PLAN = [(stage, chunk) for chunk in (0, 1) for stage in "gpotx"]


def split(table):
    high = table.astype(ml_dtypes.bfloat16)
    low = (table - high.astype(np.float64)).astype(ml_dtypes.bfloat16)
    return np.stack([high, low])


def forward_table():
    freqs = 1 + 2 * np.arange(Z)[None, :, None] + np.arange(2)[:, None, None]
    phases = freqs * np.arange(64) % 64 * (2.0 * math.pi / 64)
    return split(np.stack([np.cos(phases), -np.sin(phases)])).reshape(128, 64)


def lag_table(windows):
    freqs = 1 + 2 * np.arange(Z)[None, :] + np.arange(2)[:, None]
    phases = (np.arange(64) - 32)[:, None, None] * freqs % 64 * (2.0 * math.pi / 64)
    weights = np.where(freqs == 32, 1.0, 2.0) / windows
    table = split(np.stack([weights * np.cos(phases), weights * np.sin(phases)]))
    return np.repeat(table.reshape(4, 64, 32), 16, axis=2)


def place():
    pair, stack = lax.axis_index("pair"), lax.axis_index("stack")
    core = lax.rem(pair, 2)
    z_hi = lax.rem(lax.div(pair, 2), 2)
    return lax.div(pair, 4), lax.div(stack, ZL), z_hi * ZL + lax.rem(stack, ZL), core


def device(x, y, z, core):
    return (x * 4 + lax.div(z, ZL) * 2 + core, y * ZL + lax.rem(z, ZL))


def turn(index, by, size):
    return lax.rem(index + by, size)


def remote(src, dst, send, recv, to):
    return pltpu.make_async_remote_copy(
        src_ref=src, dst_ref=dst, send_sem=send, recv_sem=recv, device_id=to, device_id_type=MESH
    )


def local(src, dst, sem):
    return pltpu.make_async_copy(src, dst, sem)


def drain(ref, sem):
    pltpu.make_async_copy(ref, ref, sem).wait()


def whiten(raw, valid, tables, mixed, spec):
    table = tables[4, :, :128].astype(jnp.bfloat16)
    table = jnp.concatenate([table[:, :64], table[:, 64:]], axis=0)
    lanes = lax.broadcasted_iota(jnp.int32, (32, 128), 1)
    for w in range(16):
        both = jnp.dot(table, raw[w], preferred_element_type=jnp.float32)
        spectra = both[:64] + both[64:]
        re, im = spectra[:32], spectra[32:]
        power = jnp.sum(re * re + im * im, axis=1, keepdims=True) * (1.0 / 256)
        gain = lax.rsqrt(power + epsilon) * valid[0, w].astype(jnp.float32)
        re, im = re * gain, im * gain
        for half in range(2):
            a, b = re[:, 128 * half:128 * (half + 1)], im[:, 128 * half:128 * (half + 1)]
            mixed[pl.ds(32 * half + w, 32, stride=64), :] = jnp.where(lanes < 64, a, pltpu.roll(b, 64, 1))
            mixed[pl.ds(32 * half + 16 + w, 32, stride=64), :] = jnp.where(lanes < 64, pltpu.roll(a, 64, 1), b)
    spec[...] = mixed[...].reshape(2, Z, 4, 16, 128).astype(jnp.bfloat16)


def spread_table(tables, chunk, spread):
    column = lax.rem(lax.broadcasted_iota(jnp.int32, (64, 256), 1), 16)
    for row in range(16):
        keep = jnp.where(column == row, 1.0, 0.0).astype(jnp.bfloat16)
        for kind in range(4):
            spread[kind, pl.ds(64 * row, 64), :] = tables[kind, :, 256 * chunk:256 * (chunk + 1)].astype(jnp.bfloat16) * keep


def lag_sum(got, spread, half):
    def rows(g):
        groups = [got[z * X + g, pl.ds(16 * half, 16), :] for z in range(Z)]
        return jnp.concatenate(groups, axis=0)

    groups = [rows(g) for g in range(4)]
    real = jnp.concatenate([g[:, :64] for g in groups], axis=1)
    imag = jnp.concatenate([g[:, 64:] for g in groups], axis=1)
    dot = partial(jnp.dot, preferred_element_type=jnp.float32)
    return (dot(spread[0], real) + dot(spread[1], imag)) + (dot(spread[2], real) + dot(spread[3], imag))


def kernel(partners_hbm, valid_hbm, raw_hbm, tables_hbm, out, partners, valid, tables,
                    got_0, got_1, spread_0, spread_1, lagged, result, raw, mixed,
                    spec, landed, rows, cols_0, cols_1, parts, z_send, z_recv, xa_send, xa_recv, ya_send,
                    ya_recv, xg_send, xg_recv, yg_send, yg_recv, xf_send,
                    xf_recv, yf_send, yf_recv, c_send, c_recv, o_send, o_recv, here_z,
                    here_x, here_y, here_o, fetched, stored):
    x, y, z, core = place()
    cols, outs, spread = (cols_0, cols_1), (got_0, got_1), (spread_0, spread_1)
    z_hi, z_lo = lax.div(z, ZL), lax.rem(z, ZL)
    xs = [device(turn(x, d, X), y, z, core) for d in range(1, X)]
    ys = [device(x, turn(y, d, Y), z, core) for d in range(1, Y)]
    twin = device(x, y, z, 1 - core)

    fetches = [local(*pair, fetched.at[n]) for n, pair in enumerate(
        [(raw_hbm, raw), (tables_hbm, tables), (valid_hbm, valid), (partners_hbm, partners)])]
    for fetch in fetches:
        fetch.start()
    barrier = pltpu.get_barrier_semaphore()
    peers = [device(x, y, turn(z, by, Z), core) for by in ORDER[::-1]] + xs + ys + [twin]
    for peer in peers:
        pl.semaphore_signal(barrier, inc=1, device_id=peer, device_id_type=MESH)
    for fetch in fetches:
        fetch.wait()
    whiten(raw, valid, tables, mixed, spec)
    pl.semaphore_wait(barrier, len(peers))

    piece = lax.div(z, DEPTH)

    def to_plane(chunk):
        local(spec.at[chunk, z], landed.at[chunk, z], here_z.at[chunk]).start()
        for by in ORDER:
            to = turn(z, by, Z)
            remote(spec.at[chunk, to], landed.at[chunk, z], z_send.at[chunk],
                   z_recv.at[chunk, piece], device(x, y, to, core)).start()

    to_plane(0)

    def part_of(q):
        if PIECES == 1:
            return slice(None), slice(None)
        if PIECES == 2:
            return q, slice(None)
        return lax.div(q, 2), pl.ds(lax.rem(q, 2) * DEPTH, DEPTH)

    def to_groups(chunk, step):
        q = turn(piece, step, PIECES)
        hi, lo = part_of(q)
        zs = pl.ds(q * DEPTH, DEPTH)
        if step == 0:
            drain(landed.at[chunk, pl.ds(0, DEPTH - 1)], z_recv.at[chunk, q])
            drain(landed.at[chunk, 0], here_z.at[chunk])
        else:
            drain(landed.at[chunk, zs], z_recv.at[chunk, q])
        for d in range(1, 4):
            tx, ty = turn(x, d, X), turn(y, d, Y)
            remote(landed.at[chunk, zs, tx], cols[chunk].at[x, hi, core, y, lo],
                   xa_send.at[chunk], xa_recv.at[chunk, step], xs[d - 1]).start()
            remote(landed.at[chunk, zs, ty], rows.at[chunk, x, hi, y, lo],
                   ya_send.at[chunk], ya_recv.at[chunk, step], ys[d - 1]).start()
        local(landed.at[chunk, zs, x], cols[chunk].at[x, hi, core, y, lo], here_x.at[chunk, step]).start()
        local(landed.at[chunk, zs, y], rows.at[chunk, x, hi, y, lo], here_y.at[chunk, step]).start()

    def to_planes(chunk, step):
        hi, lo = part_of(turn(piece, step, PIECES))
        drain(cols[chunk].at[pl.ds(0, 3), hi, core, y, lo], xa_recv.at[chunk, step])
        drain(cols[chunk].at[0, hi, core, y, lo], here_x.at[chunk, step])
        part = cols[chunk].at[:, hi, core, y, lo]
        for side in range(2):
            remote(part, part, yg_send.at[chunk], yg_recv.at[chunk, step, side], ys[2 * side]).start()
        remote(part, part, c_send.at[chunk], c_recv.at[chunk, step], twin).start()
        drain(rows.at[chunk, x, hi, pl.ds(0, 3), lo], ya_recv.at[chunk, step])
        drain(rows.at[chunk, x, hi, 0, lo], here_y.at[chunk, step])
        part = rows.at[chunk, x, hi, :, lo]
        for side in range(2):
            remote(part, part, xg_send.at[chunk], xg_recv.at[chunk, step, side], xs[2 * side]).start()

    def onward(chunk, step):
        hi, lo = part_of(turn(piece, step, PIECES))
        for side in range(2):
            came = turn(y, 3 - 2 * side, Y)
            part = cols[chunk].at[:, hi, core, came, lo]
            drain(part, yg_recv.at[chunk, step, side])
            part = cols[chunk].at[pl.ds(2 * side, 2), hi, core, came, lo]
            remote(part, part, yf_send.at[chunk], yf_recv.at[chunk, step, side], ys[2 * side]).start()
        for side in range(2):
            came = turn(x, 3 - 2 * side, X)
            part = rows.at[chunk, came, hi, :, lo]
            drain(part, xg_recv.at[chunk, step, side])
            part = rows.at[chunk, came, hi, pl.ds(2 * side, 2), lo]
            remote(part, part, xf_send.at[chunk], xf_recv.at[chunk, step, side], xs[2 * side]).start()
        for side in range(2):
            part = cols[chunk].at[:, hi, core, turn(y, 3 - 2 * side, Y), lo]
            remote(part, part, c_send.at[chunk], c_recv.at[chunk, step], twin).start()

    def to_twin(chunk, step):
        hi, lo = part_of(turn(piece, step, PIECES))
        for side in range(2):
            part = cols[chunk].at[pl.ds(2 * side, 2), hi, core, turn(y, 2, Y), lo]
            drain(part, yf_recv.at[chunk, step, side])
            remote(part, part, c_send.at[chunk], c_recv.at[chunk, step], twin).start()

    lanes = lax.broadcasted_iota(jnp.int32, (64, 128), 1)
    sign = jnp.where(lanes < 64, 1.0, -1.0).astype(jnp.float32)

    def whole(chunk, p):
        return cols[chunk][lax.div(p, 4), lax.rem(lax.div(p, 2), 2), lax.rem(p, 2)].reshape(512, 128)

    def block(chunk, tx, th):
        own = rows[chunk, tx, th].reshape(512, 128)
        p = tx * 4 + th * 2 + core
        picked = jnp.concatenate([whole(chunk, partners[r, p]) for r in range(4)], axis=1)
        both = lax.dot_general(own, picked, (((0,), (0,)), ((), ())),
                               preferred_element_type=jnp.float32)
        found = []
        for r in range(4):
            at = both[:, 128 * r:128 * (r + 1)]
            part = at[:64] + sign * pltpu.roll(at[64:], 64, 1)
            found.append(part.reshape(8, 8, 128))
        first = pl.multiple_of((tx * 2 + th) * ZL, ZL)
        parts[chunk, pl.ds(first, ZL)] = jnp.concatenate(found, axis=1).astype(jnp.bfloat16)

    def cross(chunk):
        def blocks(n, carry):
            tx = turn(x, 3 - n, X)
            block(chunk, tx, 0)
            block(chunk, tx, 1)

            def send(by):
                tz = turn(z, by, Z)
                remote(parts.at[chunk, tx * Z + tz], outs[chunk].at[z * X + x], o_send.at[chunk],
                       o_recv.at[chunk], device(tx, y, tz, core)).start()

            for by in ORDER[::-1]:
                send(by)
            pl.when(n < 3)(lambda: send(0))
            return carry

        lax.fori_loop(0, X, blocks, 0)
        local(parts.at[chunk, x * Z + z], outs[chunk].at[z * X + x], here_o.at[chunk]).start()

    def ready(chunk):
        for step in STEPS:
            hi, lo = part_of(turn(piece, step, PIECES))
            for side in range(2):
                drain(rows.at[chunk, turn(x, 2, X), hi, pl.ds(2 * side, 2), lo], xf_recv.at[chunk, step, side])
            drain(cols[chunk].at[:, hi, 1 - core, :, lo], c_recv.at[chunk, step])

    work = {"g": to_groups, "p": to_planes, "o": onward, "t": to_twin}
    for stage, chunk in PLAN:
        if stage == "x":
            ready(chunk)
            cross(chunk)
        else:
            for step in STEPS:
                work[stage](chunk, step)
        if (stage, chunk) == ("g", 0):
            to_plane(1)

    for chunk in range(2):
        spread_table(tables, chunk, spread[chunk])
    for chunk in range(2):
        drain(outs[chunk].at[pl.ds(0, 63)], o_recv.at[chunk])
        drain(outs[chunk].at[0], here_o.at[chunk])
        for half in range(2):
            if chunk == 0:
                lagged[half] = lag_sum(got_0, spread_0, half)
            else:
                total = lagged[half] + lag_sum(got_1, spread_1, half)
                result[pl.ds(2 * half, 2)] = total.astype(jnp.bfloat16).reshape(2, 8, 64, 256)
                local(result.at[pl.ds(2 * half, 2)], out.at[pl.ds(2 * half, 2)], stored.at[half]).start()
        drain(spec.at[chunk, pl.ds(0, 15)], z_send.at[chunk])
        drain(landed.at[chunk, pl.ds(0, 12)], xa_send.at[chunk])
        drain(landed.at[chunk, pl.ds(0, 12)], ya_send.at[chunk])
        for sent in (xg_send, yg_send):
            drain(rows.at[chunk, pl.ds(0, 2)], sent.at[chunk])
        for sent in (xf_send, yf_send):
            drain(rows.at[chunk, 0], sent.at[chunk])
        drain(rows.at[chunk], c_send.at[chunk])
        drain(parts.at[chunk, pl.ds(0, 63)], o_send.at[chunk])
    for half in range(2):
        drain(result.at[pl.ds(2 * half, 2)], stored.at[half])


def exchange(raw, valid, partners, tables):
    hbm = pl.BlockSpec(memory_space=pltpu.HBM)
    dma = pltpu.SemaphoreType.DMA
    one, four = dma((2,)), dma((2, PIECES))
    return pl.pallas_call(
        kernel,
        out_shape=jax.ShapeDtypeStruct((4, 8, 64, 256), jnp.bfloat16),
        in_specs=[hbm] * 4,
        out_specs=hbm,
        scratch_shapes=[
            pltpu.SMEM((4, 16), jnp.int32),
            pltpu.SMEM((1, 16), jnp.int32),
            pltpu.VMEM((5, 64, 512), jnp.float32),
            pltpu.VMEM((Z * X, 32, 128), jnp.bfloat16),
            pltpu.VMEM((Z * X, 32, 128), jnp.bfloat16),
            pltpu.VMEM((4, 1024, 256), jnp.bfloat16),
            pltpu.VMEM((4, 1024, 256), jnp.bfloat16),
            pltpu.VMEM((2, 1024, 256), jnp.float32),
            pltpu.VMEM((4, 8, 64, 256), jnp.bfloat16),
            pltpu.VMEM((16, 64, 256), jnp.bfloat16),
            pltpu.VMEM((2048, 128), jnp.float32),
            pltpu.VMEM((2, Z, 4, 16, 128), jnp.bfloat16),
            pltpu.VMEM((2, Z, 4, 16, 128), jnp.bfloat16),
            pltpu.VMEM((2, X, 2, Y, ZL, 16, 128), jnp.bfloat16),
            pltpu.VMEM((X, 2, CORES, Y, ZL, 16, 128), jnp.bfloat16),
            pltpu.VMEM((X, 2, CORES, Y, ZL, 16, 128), jnp.bfloat16),
            pltpu.VMEM((2, 64, 32, 128), jnp.bfloat16),
        ] + [one, four] * 3 + [one, dma((2, PIECES, 2))] * 4 + [one, four] + [one, one, one, four, four, one, dma((4,)), one],
        compiler_params=pltpu.CompilerParams(
            collective_id=0, has_side_effects=True, vmem_limit_bytes=62 << 20
        ),
        cost_estimate=pl.CostEstimate(flops=1 << 30, bytes_accessed=9 << 20, transcendentals=0),
    )(partners, valid.T, raw, tables)


def copy_kernel(src, out, held, sems):
    takes = [local(src.at[r], held.at[r], sems.at[r]) for r in range(4)]
    gives = [local(held.at[r], out.at[r], sems.at[r + 4]) for r in range(4)]
    for take in takes:
        take.start()
    for take, give in zip(takes, gives):
        take.wait()
        give.start()
    for give in gives:
        give.wait()


def hand_over(lagged):
    hbm = pl.BlockSpec(memory_space=pltpu.HBM)
    return pl.pallas_call(
        copy_kernel,
        out_shape=jax.ShapeDtypeStruct((4, 8, 64, 256), jnp.bfloat16),
        in_specs=[hbm],
        out_specs=hbm,
        scratch_shapes=[pltpu.VMEM((4, 8, 64, 256), jnp.bfloat16), pltpu.SemaphoreType.DMA((8,))],
        compiler_params=pltpu.CompilerParams(vmem_limit_bytes=62 << 20),
        cost_estimate=pl.CostEstimate(flops=0, bytes_accessed=2 << 20, transcendentals=0),
    )(lagged)


def shards(raw, valid, partners):
    tables = np.zeros((5, 64, 512), np.float32)
    tables[:4] = lag_table(512)
    tables[4, :, :128] = np.concatenate(np.split(forward_table(), 2), axis=1)
    tables = jnp.asarray(tables)
    return hand_over(exchange(raw, valid, partners, tables))


def solution(mesh):
    return jax.shard_map(
        shards,
        mesh=mesh,
        in_specs=(P("stack", None, "pair"), P("stack", "pair"), P()),
        out_specs=P(None, ("pair", "stack"), None, None),
        check_vma=False,
    )
```
